512 devices in a mesh: dx: 8 (over z), dy: 8 (over y_hi, x), dz: 8 (over y_lo, core).
Axes of the slice: x: 4, y: 8 (y_hi: 2, y_lo: 4; y = y_hi * 4 + y_lo), z: 8, core: 2. Of those that a mesh axis runs over, the one named last changes fastest.
Arguments:
- node_state: bfloat16 [16, 16, 16, 32, 128], P('dx', 'dy', 'dz'), may hold values from -6 to 6
- mesh_base: int32 [3, 16, 16, 16, 32], P(None, 'dx', 'dy', 'dz'), may hold values from 0 to 255, as said below
- mesh_frac: float32 [3, 16, 16, 16, 32], P(None, 'dx', 'dy', 'dz'), may hold values from 0 to 1
- charge: float32 [16, 16, 16, 32], P('dx', 'dy', 'dz'), may hold values from -0.5 to 0.5
- nbr_code: int32 [16, 16, 16, 32, 128], P('dx', 'dy', 'dz'), may hold values from 0 to 863, as said below
- nbr_count: int32 [16, 16, 16, 32], P('dx', 'dy', 'dz'), may hold values from 32 to 128, as said below
- radial_weight: float32 [8, 128], replicated, may hold values from -2 to 2
- mix_weight: bfloat16 [3, 128, 128], replicated, may hold values from -0.5 to 0.5
- force_weight: float32 [128], replicated, may hold values from -0.5 to 0.5
Outputs:
- node_next: bfloat16 [16, 16, 16, 32, 128], P('dx', 'dy', 'dz')
- forces: float32 [3, 16, 16, 16, 32], P(None, 'dx', 'dy', 'dz')
The draws below stay inside these ranges and needn't reach their ends.
Inputs may be any that keep to these rules, and one draw needn't show every extreme that they name: `mesh_base`: entry d of an atom in octant (X, Y, Z) lies in the atom's octant: from 32 / 2 times its octant index along d up to 16 more, exclusive. In every octant the first atom sits at the lower end and the second at the upper end in every dimension. `nbr_code`: The first atom of every octant has the largest code in its first slot and 0 in its second. `nbr_count`: slots from the count on are padding. The first atom of every octant has 128 live slots, the second 128 // 4.
All inputs are finite; a program needn't handle non-finite values.
Results may differ from the reference program's by a relative error of at most 0.00095.
The reference program's roundings to bfloat16 on the way (of `edge_values` and `message`) count: a program that leaves them out, or rounds other values in their place, can miss the bound.
Values may be sent and summed in bfloat16 or wider, within the bound.
A program may use at most 64 MiB of HBM per device.

```python
import math
import jax
import jax.numpy as jnp
from jax import lax

C = 128
NB = 8
NBR = 128
OCT = 32
MB = 32
KZW = 8
MX = 256
MY = 256
MZ = 256
N_DX = 8
N_DY = 8
N_DZ = 8


def draw_mesh_base(key, part):
    half_block = MB // 2
    full_shape = (3, 2 * N_DX, 2 * N_DY, 2 * N_DZ, OCT)
    inside = jax.random.randint(jax.random.fold_in(key, 11), full_shape, 0, half_block, dtype=jnp.int32)
    inside = inside.at[:, :, :, :, 0].set(0)
    inside = inside.at[:, :, :, :, 1].set(half_block - 1)
    octant_x = jnp.broadcast_to(jnp.arange(2 * N_DX, dtype=jnp.int32)[:, None, None, None], full_shape[1:])
    octant_y = jnp.broadcast_to(jnp.arange(2 * N_DY, dtype=jnp.int32)[None, :, None, None], full_shape[1:])
    octant_z = jnp.broadcast_to(jnp.arange(2 * N_DZ, dtype=jnp.int32)[None, None, :, None], full_shape[1:])
    octant = jnp.stack([octant_x, octant_y, octant_z])
    return octant * half_block + inside


def draw_nbr_code(key, part):
    full_shape = (2 * N_DX, 2 * N_DY, 2 * N_DZ, OCT, NBR)
    side_code = jax.random.randint(jax.random.fold_in(key, 13), full_shape, 0, 27, dtype=jnp.int32)
    slot_code = jax.random.randint(jax.random.fold_in(key, 17), full_shape, 0, OCT, dtype=jnp.int32)
    own_slot = jnp.arange(OCT, dtype=jnp.int32)[:, None]
    clashes = (side_code == 13) & (slot_code == own_slot)
    slot_code = jnp.where(clashes, (slot_code + 1) % OCT, slot_code)
    code_rows = side_code * OCT + slot_code
    code_rows = code_rows.at[:, :, :, 0, 0].set(27 * OCT - 1)
    return code_rows.at[:, :, :, 0, 1].set(0)


def draw_nbr_count(key, part):
    full_shape = (2 * N_DX, 2 * N_DY, 2 * N_DZ, OCT)
    counts = jax.random.randint(jax.random.fold_in(key, 19), full_shape, NBR // 4, NBR + 1, dtype=jnp.int32)
    counts = counts.at[:, :, :, 0].set(NBR)
    return counts.at[:, :, :, 1].set(NBR // 4)


def block_levels(own_key, shape, pieces, least, largest):
    loudness, own = 1.0, jax.random.fold_in(own_key, 6)
    for axis_at, parts in pieces:
        draws = jnp.exp(jax.random.uniform(jax.random.fold_in(own, axis_at), (parts,), jnp.float32, least / len(pieces), largest / len(pieces)))
        loudness = loudness * jnp.repeat(draws, shape[axis_at] // parts).reshape([-1 if axis == axis_at else 1 for axis in range(len(shape))])
    return loudness


def centred(stream_key, shape, spread, limit, cuts=(), held_as=jnp.bfloat16):
    drawn = spread * jax.random.normal(stream_key, shape, jnp.float32)
    if cuts:
        drawn = drawn * block_levels(stream_key, shape, cuts, -0.22, 0.18)
    return jnp.clip(drawn, -limit, limit).astype(held_as)


def setup_inputs(seed: int = 0) -> dict:
    key_of = jax.random.split(jax.random.key(seed), 10)
    return {
        "node_state": centred(key_of[0], (2 * N_DX, 2 * N_DY, 2 * N_DZ, OCT, C), 1.0, 6.0, ((0, 8), (1, 8), (2, 8))),
        "mesh_base": draw_mesh_base(jax.random.fold_in(key_of[9], 71), 0),
        "mesh_frac": jnp.clip(1.0 * jax.random.uniform(key_of[2], (3, 2 * N_DX, 2 * N_DY, 2 * N_DZ, OCT), jnp.float32) ** block_levels(key_of[2], (3, 2 * N_DX, 2 * N_DY, 2 * N_DZ, OCT), ((1, 8), (2, 8), (3, 8)), -0.2, 0.2), 0.0, 1.0),
        "charge": jnp.clip(jax.random.uniform(key_of[3], (2 * N_DX, 2 * N_DY, 2 * N_DZ, OCT), jnp.float32, -0.5, 0.5) * block_levels(key_of[3], (2 * N_DX, 2 * N_DY, 2 * N_DZ, OCT), ((0, 8), (1, 8), (2, 8)), -0.4, 0.0), -0.5, 0.5),
        "nbr_code": draw_nbr_code(jax.random.fold_in(key_of[9], 71), 0),
        "nbr_count": draw_nbr_count(jax.random.fold_in(key_of[9], 71), 0),
        "radial_weight": centred(key_of[6], (NB, C), NB ** -0.5, 2.0, (), jnp.float32),
        "mix_weight": centred(key_of[7], (3, C, C), C ** -0.5, 0.5),
        "force_weight": centred(key_of[8], (C,), C ** -0.5, 0.5, (), jnp.float32),
    }


cell_size = 1.13
ewald_beta = 0.625
coulomb = 332.0637
sigma_low = 8.0
sigma_rate = 1.5
highest = lax.Precision.HIGHEST

def spline_terms(fraction):
    remainder = 1.0 - fraction
    frac_square = fraction * fraction
    frac_cube = frac_square * fraction
    weights = jnp.stack([remainder * remainder * remainder / 6.0, (3.0 * frac_cube - 6.0 * frac_square + 4.0) / 6.0, (-3.0 * frac_cube + 3.0 * frac_square + 3.0 * fraction + 1.0) / 6.0, frac_cube / 6.0])
    slopes = jnp.stack([-0.5 * remainder * remainder, 1.5 * frac_square - 2.0 * fraction, -1.5 * frac_square + fraction + 0.5, 0.5 * frac_square])
    return (weights, slopes)

def harmonics(direction):
    unit_x, unit_y, unit_z = (direction[0], direction[1], direction[2])
    root_three = math.sqrt(3.0)
    root_fifteen = math.sqrt(15.0)
    root_five = math.sqrt(5.0)
    return jnp.stack([jnp.ones_like(unit_x), root_three * unit_x, root_three * unit_y, root_three * unit_z, root_fifteen * unit_x * unit_y, root_fifteen * unit_y * unit_z, 0.5 * root_five * (3.0 * unit_z * unit_z - 1.0), root_fifteen * unit_x * unit_z, 0.5 * root_fifteen * (unit_x * unit_x - unit_y * unit_y)])

def edge_terms(displace, active):
    square = lax.optimization_barrier(jnp.sum(displace * displace, axis=0))
    direction = displace / jnp.sqrt(square + 1.0)
    angular = harmonics(direction)
    distance = cell_size * jnp.sqrt(square)
    widths = sigma_low * jnp.power(sigma_rate, jnp.arange(NB).astype(jnp.float32))
    radial = jnp.exp(-jnp.square(distance[None] / widths[:, None, None]))
    products = radial[:, None] * angular[None] * active.astype(jnp.float32)[None, None]
    atom_rows = displace.shape[1]
    return jnp.transpose(products, (2, 0, 1, 3)).reshape(atom_rows, NB * 9, -1).astype(jnp.bfloat16)

def node_update(edge_values, neighbour_state, own_state, radial_weight, mix_weight, force_weight):
    summed = jnp.einsum('bkn,bnc->bkc', edge_values.astype(jnp.float32), neighbour_state.astype(jnp.float32))
    atom_rows = summed.shape[0]
    summed = summed.reshape(atom_rows, NB, 9, -1)
    message = (lax.optimization_barrier(jnp.sum(summed * radial_weight[None, :, None, :], axis=1)) / math.sqrt(NBR)).astype(jnp.bfloat16)
    scalar = jnp.dot(message[:, 0], mix_weight[0], preferred_element_type=jnp.float32)
    vector = jnp.einsum('bmc,cd->bmd', message[:, 1:4].astype(jnp.float32), mix_weight[1].astype(jnp.float32))
    tensor = jnp.einsum('bmc,cd->bmd', message[:, 4:9].astype(jnp.float32), mix_weight[2].astype(jnp.float32))
    invariant = scalar + lax.optimization_barrier(jnp.sum(tensor * tensor, axis=1))
    gating = jax.nn.sigmoid(invariant)
    updated = (own_state.astype(jnp.float32) + jax.nn.silu(invariant)).astype(jnp.bfloat16)
    short_push = lax.optimization_barrier(jnp.sum(vector * (gating * force_weight)[:, None, :], axis=2))
    return (updated, jnp.transpose(short_push))

def phases(wavenumber, cell_index, extent):
    return 2.0 * math.pi / extent * jnp.mod(wavenumber * cell_index, extent).astype(jnp.float32)

def wave_sums(coeff, start_cells, wavenumber, extent, orient):
    wave_re = jnp.zeros((start_cells.shape[0], wavenumber.shape[0]), jnp.float32)
    wave_im = jnp.zeros((start_cells.shape[0], wavenumber.shape[0]), jnp.float32)
    for stencil in range(4):
        angles = phases(wavenumber[None, :], (start_cells + stencil)[:, None], extent)
        wave_re = wave_re + coeff[stencil][:, None] * jnp.cos(angles)
        wave_im = wave_im + coeff[stencil][:, None] * jnp.sin(angles)
    return (wave_re, orient * wave_im)

def cell_table(coeff, local_cells, cell_index):
    table = jnp.zeros((local_cells.shape[0], cell_index.shape[0]), jnp.float32)
    for stencil in range(4):
        match = (cell_index[None, :] == (local_cells + stencil)[:, None]).astype(jnp.float32)
        table = table + coeff[stencil][:, None] * match
    return table

def influence(modes_x, modes_y, modes_z, length_x, length_y, length_z):

    def folded(wavenumber, extent):
        return jnp.where(2 * wavenumber >= extent, wavenumber - extent, wavenumber).astype(jnp.float32) / (cell_size * extent)
    wave_square = jnp.square(folded(modes_x, length_x)) + jnp.square(folded(modes_y, length_y)) + jnp.square(folded(modes_z, length_z))
    volume = cell_size ** 3 * length_x * length_y * length_z
    return coulomb / (math.pi * volume) * jnp.exp(-math.pi ** 2 * wave_square / ewald_beta ** 2) / wave_square

def projected(value_re, value_im, wave_y_re, wave_y_im, wave_z_re, wave_z_im):
    inner_re = lax.optimization_barrier(jnp.sum(value_re * wave_y_re[:, :, None] - value_im * wave_y_im[:, :, None], axis=1))
    inner_im = lax.optimization_barrier(jnp.sum(value_re * wave_y_im[:, :, None] + value_im * wave_y_re[:, :, None], axis=1))
    return 2.0 * lax.optimization_barrier(jnp.sum(inner_re * wave_z_re - inner_im * wave_z_im, axis=1))

def short_range(node_state, places, nbr_code, nbr_count, radial_weight, mix_weight, force_weight):
    wide_x = 2 * N_DX
    wide_y = 2 * N_DY
    wide_z = 2 * N_DZ
    half_block = MB // 2
    columns = wide_x * wide_y
    block_rows = wide_z * OCT
    flat_state = node_state.reshape(-1, C)
    flat_places = places.reshape(3, -1)
    code_table = nbr_code.reshape(columns, block_rows, NBR)
    count_table = nbr_count.reshape(columns, block_rows)
    state_table = node_state.reshape(columns, block_rows, C)
    z_octant = jnp.arange(block_rows, dtype=jnp.int32) // OCT
    slot_index = jnp.arange(NBR, dtype=jnp.int32)

    def one_column(column):
        code_rows = code_table[column]
        count_rows = count_table[column]
        side_code = code_rows // OCT
        slot_code = code_rows % OCT
        reach_x = column // wide_y + side_code // 9 - 1
        reach_y = column % wide_y + side_code // 3 % 3 - 1
        reach_z = z_octant[:, None] + side_code % 3 - 1
        wrapped_x = jnp.mod(reach_x, wide_x)
        wrapped_y = jnp.mod(reach_y, wide_y)
        wrapped_z = jnp.mod(reach_z, wide_z)
        wrap_shift = jnp.stack([(reach_x - wrapped_x) * half_block, (reach_y - wrapped_y) * half_block, (reach_z - wrapped_z) * half_block]).astype(jnp.float32)
        neighbour = ((wrapped_x * wide_y + wrapped_y) * wide_z + wrapped_z) * OCT + slot_code
        own_index = column * block_rows + jnp.arange(block_rows, dtype=jnp.int32)
        own_places = flat_places[:, own_index]
        displace = flat_places[:, neighbour] + wrap_shift - own_places[:, :, None]
        active = slot_index[None, :] < count_rows[:, None]
        edge_values = edge_terms(displace, active)
        return node_update(edge_values, flat_state[neighbour], state_table[column], radial_weight, mix_weight, force_weight)
    return lax.map(one_column, jnp.arange(columns, dtype=jnp.int32))

def long_range(mesh_base, mesh_frac, charge):
    half_block = MB // 2
    span_x = half_block + 3
    wide_y = 2 * N_DY
    columns = 2 * N_DX * wide_y
    block_rows = 2 * N_DZ * OCT
    flat_base = mesh_base.reshape(3, columns, block_rows)
    flat_frac = mesh_frac.reshape(3, columns, block_rows)
    flat_charge = charge.reshape(columns, block_rows)
    mode_count = MY * KZW
    modes_y = jnp.arange(MY, dtype=jnp.int32)
    planes = 1 + jnp.arange(KZW, dtype=jnp.int32)
    span_cells = jnp.arange(span_x, dtype=jnp.int32)

    def column_setup(column):
        base_now = flat_base[:, column]
        weights, slopes = spline_terms(flat_frac[:, column])
        first_x = column // wide_y * half_block
        local_x = base_now[0] - first_x
        return (base_now, weights, slopes, first_x, local_x)

    def forward(carried, column):
        base_now, weights, slopes, first_x, local_x = column_setup(column)
        charges_now = flat_charge[column]
        table_x = cell_table(weights[:, 0], local_x, span_cells)
        wave_y_re, wave_y_im = wave_sums(weights[:, 1], base_now[1], modes_y, MY, -1.0)
        wave_z_re, wave_z_im = wave_sums(weights[:, 2], base_now[2], planes, MZ, -1.0)
        mixed_re = (wave_y_re[:, :, None] * wave_z_re[:, None, :] - wave_y_im[:, :, None] * wave_z_im[:, None, :]).reshape(-1, mode_count)
        mixed_im = (wave_y_re[:, :, None] * wave_z_im[:, None, :] + wave_y_im[:, :, None] * wave_z_re[:, None, :]).reshape(-1, mode_count)
        left_side = jnp.transpose(table_x * charges_now[:, None])
        part_re = jnp.dot(left_side, mixed_re, precision=highest)
        part_im = jnp.dot(left_side, mixed_im, precision=highest)
        row_ids = jnp.mod(first_x + span_cells, MX)
        slab_re, slab_im = carried
        return ((slab_re.at[row_ids].add(part_re), slab_im.at[row_ids].add(part_im)), None)
    initial = (jnp.zeros((MX, mode_count), jnp.float32), jnp.zeros((MX, mode_count), jnp.float32))
    (slab_re, slab_im), _ = lax.scan(forward, initial, jnp.arange(columns, dtype=jnp.int32))
    modes_x = jnp.arange(MX, dtype=jnp.int32)
    angle_x = phases(modes_x[:, None], modes_x[None, :], MX)
    cos_x = jnp.cos(angle_x)
    sin_x = jnp.sin(angle_x)
    spec_re = jnp.dot(cos_x.T, slab_re, precision=highest) + jnp.dot(sin_x.T, slab_im, precision=highest)
    spec_im = jnp.dot(cos_x.T, slab_im, precision=highest) - jnp.dot(sin_x.T, slab_re, precision=highest)
    green_table = influence(modes_x[:, None, None], modes_y[None, :, None], planes[None, None, :], MX, MY, MZ).reshape(MX, mode_count)
    scaled_re = green_table * spec_re
    scaled_im = green_table * spec_im
    back_re = jnp.dot(cos_x, scaled_re, precision=highest) - jnp.dot(sin_x, scaled_im, precision=highest)
    back_im = jnp.dot(sin_x, scaled_re, precision=highest) + jnp.dot(cos_x, scaled_im, precision=highest)

    def backward(column):
        base_now, weights, slopes, first_x, local_x = column_setup(column)
        charges_now = flat_charge[column]
        row_ids = jnp.mod(first_x + span_cells, MX)
        near_re = back_re[row_ids]
        near_im = back_im[row_ids]
        table_x = cell_table(weights[:, 0], local_x, span_cells)
        slope_x = cell_table(slopes[:, 0], local_x, span_cells)
        value_re = jnp.dot(table_x, near_re, precision=highest).reshape(-1, MY, KZW)
        value_im = jnp.dot(table_x, near_im, precision=highest).reshape(-1, MY, KZW)
        tilt_re = jnp.dot(slope_x, near_re, precision=highest).reshape(-1, MY, KZW)
        tilt_im = jnp.dot(slope_x, near_im, precision=highest).reshape(-1, MY, KZW)
        wave_y = wave_sums(weights[:, 1], base_now[1], modes_y, MY, 1.0)
        slope_y = wave_sums(slopes[:, 1], base_now[1], modes_y, MY, 1.0)
        wave_z = wave_sums(weights[:, 2], base_now[2], planes, MZ, 1.0)
        slope_z = wave_sums(slopes[:, 2], base_now[2], planes, MZ, 1.0)
        grad_x = projected(tilt_re, tilt_im, wave_y[0], wave_y[1], wave_z[0], wave_z[1])
        grad_y = projected(value_re, value_im, slope_y[0], slope_y[1], wave_z[0], wave_z[1])
        grad_z = projected(value_re, value_im, wave_y[0], wave_y[1], slope_z[0], slope_z[1])
        return -(charges_now / cell_size) * jnp.stack([grad_x, grad_y, grad_z])
    return lax.map(backward, jnp.arange(columns, dtype=jnp.int32))

def reference(node_state, mesh_base, mesh_frac, charge, nbr_code, nbr_count, radial_weight, mix_weight, force_weight):
    places = mesh_base.astype(jnp.float32) + mesh_frac
    updated, short_push = short_range(node_state, places, nbr_code, nbr_count, radial_weight, mix_weight, force_weight)
    long_push = long_range(mesh_base, mesh_frac, charge)
    node_next = updated.reshape(node_state.shape)
    forces = jnp.transpose(short_push + long_push, (1, 0, 2)).reshape(3, 2 * N_DX, 2 * N_DY, 2 * N_DZ, OCT)
    return (node_next, forces)
```

```python
import functools
import math

import jax
import jax.numpy as jnp
import numpy as np
from jax import lax
from jax.experimental import pallas as pl
from jax.experimental.pallas import tpu as pltpu
from jax.sharding import PartitionSpec as P

NB = 8
NBR = 128
MB = 32
KZW = 8
OCT = 32
ATOMS = 8 * OCT
WIN = 40
EXT = 256

cell_size = 1.13
ewald_beta = 0.625
coulomb = 332.0637
sigma_low = 8.0
sigma_rate = 1.5
highest = lax.Precision.HIGHEST
MESH = pl.DeviceIdType.MESH
f32 = jnp.float32
bf16 = jnp.bfloat16


def wave_tables():
    cells = np.arange(WIN)
    angle = 2.0 * np.pi / EXT
    table_z = np.zeros((8, WIN, KZW, 2, 64))
    table_y = np.zeros((8, 2, 64, 8, 2, 64))
    back_x = np.zeros((8, 2, WIN, EXT))
    modes = np.arange(EXT)
    for d in range(8):
        at = d * MB + cells
        turn = angle * np.mod(at[:, None] * (1 + np.arange(KZW))[None, :], EXT)
        table_z[d, :, :, 0] = np.cos(turn)[:, :, None]
        table_z[d, :, :, 1] = -np.sin(turn)[:, :, None]
        turn = (angle * np.mod(at[:, None] * modes[None, :], EXT)).reshape(WIN, 8, 32)
        table_y[d, 0, :WIN, :, 0, :32] = np.cos(turn)
        table_y[d, 0, :WIN, :, 1, :32] = -np.sin(turn)
        table_y[d, 1, :WIN, :, 0, :32] = np.sin(turn)
        table_y[d, 1, :WIN, :, 1, :32] = np.cos(turn)
        turn = angle * np.mod(at[:, None] * modes[None, :], EXT)
        back_x[d, 0] = np.cos(turn)
        back_x[d, 1] = np.sin(turn)
    turn = angle * np.mod(modes[:, None] * modes[None, :], EXT)
    fore_x = np.stack([np.cos(turn), np.sin(turn)])
    return (
        table_z.reshape(8, WIN, KZW * 128).astype(np.float32),
        table_y.reshape(8, 128, 1024).astype(np.float32),
        fore_x.astype(np.float32),
        back_x.astype(np.float32),
    )


def dot_full(a, b):
    return jnp.dot(a, b, precision=highest, preferred_element_type=f32)


def spline_tables(base, frac, cell):
    left = 1.0 - frac
    square = frac * frac
    cube = square * frac
    weights = (
        left * left * left / 6.0,
        (3.0 * cube - 6.0 * square + 4.0) / 6.0,
        (-3.0 * cube + 3.0 * square + 3.0 * frac + 1.0) / 6.0,
        cube / 6.0,
    )
    slopes = (
        -0.5 * left * left,
        1.5 * square - 2.0 * frac,
        -1.5 * square + frac + 0.5,
        0.5 * square,
    )
    offset = cell - base
    table = jnp.zeros_like(offset)
    slope = jnp.zeros_like(offset)
    for t in range(4):
        hit = offset == float(t)
        table = jnp.where(hit, weights[t], table)
        slope = jnp.where(hit, slopes[t], slope)
    return table, slope


def mesh_kernel(
    state, pos, cols, tz_all, ty_all, fx, bx_all,
    hs, hp, grads,
    tz, ty, bx, wz, dwz, xt, yt, ys,
    s1, r1, s2, r2, s3, r3, s4, r4, s5, r5, grid,
    send_sem, recv_sem, hsend, hrecv, lsem,
):
    ix, iy, iz = lax.axis_index("dx"), lax.axis_index("dy"), lax.axis_index("dz")
    here = {"dx": ix, "dy": iy, "dz": iz}
    barrier = pltpu.get_barrier_semaphore()

    for axis in ("dx", "dy", "dz"):

        def greet(s, carry, axis=axis):
            pl.semaphore_signal(
                barrier, inc=1, device_id={axis: lax.rem(here[axis] + s, 8)}, device_id_type=MESH
            )
            return carry

        lax.fori_loop(1, 8, greet, 0)

    local = [
        pltpu.make_async_copy(tz_all.at[iz], tz, lsem.at[0]),
        pltpu.make_async_copy(ty_all.at[iy], ty, lsem.at[1]),
        pltpu.make_async_copy(bx_all.at[ix], bx, lsem.at[2]),
        pltpu.make_async_copy(state, hs.at[pl.ds(1, 2), pl.ds(1, 2), pl.ds(1, 2)], lsem.at[3]),
        pltpu.make_async_copy(pos, hp.at[pl.ds(1, 2), pl.ds(1, 2), pl.ds(1, 2)], lsem.at[4]),
    ]
    for copy in local:
        copy.start()

    lane = lax.broadcasted_iota(jnp.int32, (ATOMS, 128), 1)
    cell = lane.astype(f32)
    half_cell = (lane % 64).astype(f32)

    def column(c):
        return jnp.broadcast_to(cols[:, c : c + 1], (ATOMS, 128))

    table, slope = spline_tables(column(2), column(5), cell)
    local[0].wait()
    wz[...] = dot_full(table[:, :WIN], tz[...])
    dwz[...] = dot_full(slope[:, :WIN], tz[...])
    table, slope = spline_tables(column(1), column(4), half_cell)
    yt[...] = table
    ys[...] = slope
    table, slope = spline_tables(column(0), column(3), cell)
    xt[0:ATOMS] = table
    xt[ATOMS : 2 * ATOMS] = slope
    left = jnp.transpose(table * column(6))[:WIN]
    for k in range(KZW):
        s1[k] = dot_full(left, yt[...] * wz[:, k * 128 : (k + 1) * 128])

    pl.semaphore_wait(barrier, 21)

    def halo(stage, axis, src_up, dst_up, src_down, dst_down):
        out = []
        for which in range(2):
            full = (hs, hp)[which]
            first = (state, pos)[which]
            up_src = first.at[src_up] if stage == 0 else full.at[src_up]
            down_src = first.at[src_down] if stage == 0 else full.at[src_down]
            for way, (src, dst, step) in enumerate(
                ((up_src, full.at[dst_up], 1), (down_src, full.at[dst_down], 7))
            ):
                n = stage * 4 + which * 2 + way
                out.append(
                    pltpu.make_async_remote_copy(
                        src_ref=src,
                        dst_ref=dst,
                        send_sem=hsend.at[n],
                        recv_sem=hrecv.at[n],
                        device_id={axis: lax.rem(here[axis] + step, 8)},
                        device_id_type=MESH,
                    )
                )
        return out

    mid = pl.ds(1, 2)
    full = pl.ds(0, 4)

    def one(n):
        return pl.ds(n, 1)

    halo_x = halo(0, "dx", (one(1),), (one(0), mid, mid), (one(0),), (one(3), mid, mid))
    halo_y = halo(
        1, "dy", (full, one(2), mid), (full, one(0), mid), (full, one(1), mid), (full, one(3), mid)
    )
    halo_z = halo(
        2, "dz", (full, full, one(2)), (full, full, one(0)), (full, full, one(1)), (full, full, one(3))
    )

    def link(phase, axis, s, src, dst):
        return pltpu.make_async_remote_copy(
            src_ref=src,
            dst_ref=dst,
            send_sem=send_sem.at[phase, s],
            recv_sem=recv_sem.at[phase, s],
            device_id={axis: lax.rem(here[axis] + s, 8)},
            device_id_type=MESH,
        )

    def deal(phase, axis, s, sent, got):
        return link(phase, axis, s, sent.at[lax.rem(here[axis] + s, 8)], got.at[s])

    def share(phase, axis, s, sent, got, arriving):
        slot = lax.rem(here[axis] + 8 - s, 8) if arriving else here[axis]
        return link(phase, axis, s, sent, got.at[slot])

    def start_deal(phase, axis, sent, got):
        def body(s, carry):
            deal(phase, axis, s, sent, got).start()
            return carry

        lax.fori_loop(1, 8, body, 0)

    def wait_deal(phase, axis, sent, got):
        def body(s, carry):
            deal(phase, axis, s, sent, got).wait()
            return carry

        lax.fori_loop(1, 8, body, 0)
        total = sent[here[axis]]
        for s in range(1, 8):
            total = total + got[s]
        return total

    def start_share(phase, axis, sent, got):
        got[here[axis]] = sent[...]

        def body(s, carry):
            share(phase, axis, s, sent, got, False).start()
            return carry

        lax.fori_loop(1, 8, body, 0)

    def wait_share(phase, axis, sent, got):
        def body(s, carry):
            share(phase, axis, s, sent, got, True).wait()
            return carry

        lax.fori_loop(1, 8, body, 0)

    start_deal(0, "dz", s1, r1)
    for copy in halo_x:
        copy.start()
    local[1].wait()
    total = wait_deal(0, "dz", s1, r1)
    spread = dot_full(total, ty[...])
    for p in range(8):
        s2[p] = spread[:, p * 128 : (p + 1) * 128]
    start_deal(1, "dy", s2, r2)
    local[3].wait()
    local[4].wait()
    for copy in halo_x:
        copy.wait()
    for copy in halo_y:
        copy.start()

    kx = lax.broadcasted_iota(jnp.int32, (EXT, 128), 0)
    lane_k = lax.broadcasted_iota(jnp.int32, (EXT, 128), 1)
    ky = iy * 32 + (lane_k % 64) % 32

    def folded(k):
        return jnp.where(2 * k >= EXT, k - EXT, k).astype(f32) / (cell_size * EXT)

    wave_z = (iz + 1).astype(f32) / (cell_size * EXT)
    wave_square = folded(kx) * folded(kx) + folded(ky) * folded(ky) + wave_z * wave_z
    volume = cell_size**3 * EXT * EXT * EXT
    green = (
        coulomb
        / (math.pi * volume)
        * jnp.exp(-(math.pi**2) / ewald_beta**2 * wave_square)
        / wave_square
    )
    sign = jnp.where(lane_k < 64, 1.0, -1.0).astype(f32)

    s3[...] = wait_deal(1, "dy", s2, r2)
    start_share(2, "dx", s3, r3)
    for copy in halo_y:
        copy.wait()
    for copy in halo_z:
        copy.start()
    local[2].wait()
    wait_share(2, "dx", s3, r3)
    for d in range(8):
        grid[d * 32 : d * 32 + 8] = r3[d, 0:8] + r3[(d + 7) % 8, 32:40]
        grid[d * 32 + 8 : d * 32 + 32] = r3[d, 8:32]
    lined = grid[...]
    spec = dot_full(fx[0], lined) + dot_full(fx[1], sign * pltpu.roll(lined, 64, 1))
    scaled = spec * green
    s4[...] = dot_full(bx[0], scaled) - dot_full(bx[1], sign * pltpu.roll(scaled, 64, 1))
    start_share(3, "dy", s4, r4)
    wait_share(3, "dy", s4, r4)
    back = jnp.zeros((WIN, 128), f32)
    for p in range(8):
        back = back + lax.dot_general(
            r4[p],
            ty[:, p * 128 : (p + 1) * 128],
            (((1,), (1,)), ((), ())),
            precision=highest,
            preferred_element_type=f32,
        )
    s5[...] = back
    start_share(4, "dz", s5, r5)
    for copy in halo_z:
        copy.wait()
    wait_share(4, "dz", s5, r5)
    along = jnp.zeros((ATOMS, 128), f32)
    along_z = jnp.zeros((ATOMS, 128), f32)
    tilted = jnp.zeros((ATOMS, 128), f32)
    for k in range(KZW):
        near = dot_full(xt[:, :WIN], r5[k])
        wave = wz[:, k * 128 : (k + 1) * 128]
        along = along + near[:ATOMS] * wave
        along_z = along_z + near[:ATOMS] * dwz[:, k * 128 : (k + 1) * 128]
        tilted = tilted + near[ATOMS:] * wave
    grad_x = jnp.sum(tilted * yt[...], axis=1, keepdims=True)
    grad_y = jnp.sum(along * ys[...], axis=1, keepdims=True)
    grad_z = jnp.sum(along_z * yt[...], axis=1, keepdims=True)
    scale = -(column(6) / cell_size) * 2.0
    grads[...] = scale * jnp.where(lane == 0, grad_x, jnp.where(lane == 1, grad_y, grad_z))


def mesh_call(state, pos, cols, tables):
    any_spec = pl.BlockSpec(memory_space=pl.ANY)
    vmem_spec = pl.BlockSpec(memory_space=pltpu.VMEM)
    block = (8, WIN, 128)
    return pl.pallas_call(
        mesh_kernel,
        out_shape=(
            jax.ShapeDtypeStruct((4, 4, 4, OCT, 128), bf16),
            jax.ShapeDtypeStruct((4, 4, 4, 8, 128), f32),
            jax.ShapeDtypeStruct((ATOMS, 128), f32),
        ),
        in_specs=[any_spec, any_spec, vmem_spec, any_spec, any_spec, vmem_spec, any_spec],
        out_specs=(any_spec, any_spec, vmem_spec),
        scratch_shapes=[
            pltpu.VMEM((WIN, 1024), f32),
            pltpu.VMEM((128, 1024), f32),
            pltpu.VMEM((2, WIN, EXT), f32),
            pltpu.VMEM((ATOMS, 1024), f32),
            pltpu.VMEM((ATOMS, 1024), f32),
            pltpu.VMEM((2 * ATOMS, 128), f32),
            pltpu.VMEM((ATOMS, 128), f32),
            pltpu.VMEM((ATOMS, 128), f32),
            pltpu.VMEM(block, f32),
            pltpu.VMEM(block, f32),
            pltpu.VMEM(block, f32),
            pltpu.VMEM(block, f32),
            pltpu.VMEM((WIN, 128), f32),
            pltpu.VMEM(block, f32),
            pltpu.VMEM((WIN, 128), f32),
            pltpu.VMEM(block, f32),
            pltpu.VMEM((WIN, 128), f32),
            pltpu.VMEM(block, f32),
            pltpu.VMEM((EXT, 128), f32),
            pltpu.SemaphoreType.DMA((5, 8)),
            pltpu.SemaphoreType.DMA((5, 8)),
            pltpu.SemaphoreType.DMA((12,)),
            pltpu.SemaphoreType.DMA((12,)),
            pltpu.SemaphoreType.DMA((5,)),
        ],
        compiler_params=pltpu.CompilerParams(
            collective_id=0, has_side_effects=True, vmem_limit_bytes=40 * 1024 * 1024
        ),
        name="mesh_forces",
    )(state, pos, cols, *tables)


def top_power(count):
    power = count
    for bit in range(1, 8):
        power = jnp.where(count >= 2.0**bit, 2.0**bit, power)
    return power


def short_kernel(
    shift, hs, hp, state, cols, codes, rw, mix, fw, grads,
    node_out, force_out,
    cand, hist, lhs, msg, total, extra, pick,
):
    lane = lax.broadcasted_iota(jnp.int32, (8, 128), 1)
    sub8 = lax.broadcasted_iota(jnp.int32, (8, 128), 0)
    sub128 = lax.broadcasted_iota(jnp.int32, (128, 128), 0)
    lane128 = lax.broadcasted_iota(jnp.int32, (128, 128), 1)
    lane32 = lax.broadcasted_iota(jnp.int32, (OCT, 128), 1)
    slot = lax.broadcasted_iota(jnp.int32, (1, 128), 1).astype(f32)
    before = jnp.where(sub128 < lane128, 1.0, 0.0).astype(bf16)
    ones = jnp.ones((128, 128), bf16)
    place_id = (sub128 & 63).astype(f32)
    root3, root5, root15 = math.sqrt(3.0), math.sqrt(5.0), math.sqrt(15.0)
    rates = [
        -(cell_size**2) / (sigma_low * sigma_rate**b) ** 2 / math.log(2.0) for b in range(NB)
    ]
    cand[864:896] = jnp.zeros((32, 128), bf16)
    extra[48:64] = jnp.zeros((16, 896), bf16)

    def one_octant(octant, carry):
        cx, cy, cz = octant // 4, octant // 2 % 2, octant % 2
        row0 = pl.multiple_of(octant * OCT, OCT)

        def count(i, c):
            row = codes[pl.ds(row0 + i, 1), :]
            live = slot < cols[pl.ds(row0 + i, 1), 10:11]
            row = jnp.where(live, row, 1023)
            high = jnp.broadcast_to(row >> 7, (8, 128))
            low = jnp.broadcast_to(row & 127, (128, 128))
            a = jnp.where(high == sub8, 1.0, 0.0).astype(bf16)
            b = jnp.where(low == sub128, 1.0, 0.0).astype(bf16)
            hist[pl.ds(pl.multiple_of(i * 8, 8), 8), :] = lax.dot_general(
                a, b, (((1,), (1,)), ((), ())), preferred_element_type=f32
            )
            return c

        lax.fori_loop(0, OCT, count, 0, unroll=8)
        own = [
            jnp.broadcast_to(cols[pl.ds(row0, OCT), 7 + d : 8 + d], (OCT, 128)) for d in range(3)
        ]
        tiles = []
        for side in range(27):
            hx, hy, hz = cx + side // 9, cy + side // 3 % 3, cz + side % 3
            cand[side * 32 : side * 32 + 32] = hs[hx, hy, hz]
            sx = shift[0, hx]
            sy = shift[1, hy]
            sz = shift[2, hz]
            tiles.append(hp[hx, hy, hz] + jnp.where(sub8 == 0, sx, jnp.where(sub8 == 1, sy, sz)))
        tiles.append(tiles[26])
        places = []
        for t in range(7):
            four = tiles[4 * t : 4 * t + 4]
            place = jnp.where(
                lane < 32, four[0], jnp.where(lane < 64, four[1], jnp.where(lane < 96, four[2], four[3]))
            )
            places.append(place)
            at = slice(t * 128, (t + 1) * 128)
            first = place.astype(bf16).astype(f32)
            rest = place - first
            second = rest.astype(bf16).astype(f32)
            extra[32:48, at] = jnp.concatenate([first, second], axis=0).astype(bf16)
            extra[48:64, at] = jnp.concatenate([rest - second, jnp.zeros_like(rest)], axis=0).astype(bf16)
        total[...] = jnp.zeros_like(total)

        def one_pass(carry):
            flags = jnp.zeros((8, 128), f32)
            for t in range(7):
                rest = jnp.maximum(hist[pl.ds(t, OCT, 8), :] - 2.0, 0.0)
                extra[0:OCT, t * 128 : (t + 1) * 128] = rest.astype(bf16)
                flag = jnp.where(jnp.max(rest, axis=0, keepdims=True) > 0.0, 1.0, 0.0)
                flags = jnp.where(sub8 == t, flag, flags)
            flags_b = flags.astype(bf16)
            rank = jnp.dot(flags_b, before, preferred_element_type=f32)
            sums = jnp.dot(flags_b, ones, preferred_element_type=f32)
            offset = jnp.zeros((1, 128), f32)
            for t in range(7):
                key = jnp.where(flags[t : t + 1] > 0.0, rank[t : t + 1] + offset, -1.0)
                pick[:, t * 128 : (t + 1) * 128] = jnp.where(key == place_id, 1.0, 0.0).astype(bf16)
                offset = offset + sums[t : t + 1]
            picked = lax.dot_general(
                extra[...], pick[...], (((1,), (1,)), ((), ())), preferred_element_type=f32
            )
            cand[896:1024] = jnp.dot(
                pick[...], cand[0:896], preferred_element_type=f32
            ).astype(bf16)
            more = picked[0:OCT]
            power = top_power(more)
            second = top_power(more - power)
            left = jnp.max(jnp.maximum(more - power - second, offset - 64.0))
            again = left > 0.0
            spare = jnp.where(lane32 < 64, power, second) * jnp.where(again, 0.0, 1.0)
            spare_place = picked[32:40] + picked[40:48] + picked[48:56]
            for t in range(8):
                place = spare_place if t == 7 else places[t]
                times_all = spare if t == 7 else jnp.minimum(hist[pl.ds(t, OCT, 8), :], 2.0)
                for h in range(2):
                    rows = slice(16 * h, 16 * h + 16)
                    delta = [place[d : d + 1] - own[d][rows] for d in range(3)]
                    square = delta[0] * delta[0] + delta[1] * delta[1] + delta[2] * delta[2]
                    inv = lax.rsqrt(square + 1.0)
                    ux, uy, uz = (d * inv for d in delta)
                    times = times_all[rows]
                    radial = [jnp.exp2(square * rates[b]) * times for b in range(NB)]
                    angular = [
                        None,
                        root3 * ux,
                        root3 * uy,
                        root3 * uz,
                        root15 * ux * uy,
                        root15 * uy * uz,
                        0.5 * root5 * (3.0 * uz * uz - 1.0),
                        root15 * ux * uz,
                        0.5 * root15 * (ux * ux - uy * uy),
                    ]
                    for lm in range(9):
                        for b in range(NB):
                            value = radial[b] if lm == 0 else radial[b] * angular[lm]
                            at = (lm * NB + b) * OCT + 16 * h
                            lhs[at : at + 16, t * 128 : (t + 1) * 128] = value.astype(bf16)
            for lm in range(9):
                summed = jnp.dot(
                    lhs[lm * 256 : (lm + 1) * 256], cand[...], preferred_element_type=f32
                )
                message = summed[0:OCT] * rw[0:1]
                for b in range(1, NB):
                    message = message + summed[b * OCT : (b + 1) * OCT] * rw[b : b + 1]
                total[lm] = total[lm] + message

            @pl.when(again)
            def _():
                for t in range(7):
                    hist[pl.ds(t, OCT, 8), :] = jnp.maximum(hist[pl.ds(t, OCT, 8), :] - 2.0, 0.0)

            return again

        lax.while_loop(lambda again: again, one_pass, jnp.bool_(True))
        for lm in range(9):
            msg[lm, pl.ds(row0, OCT), :] = (total[lm] * (1.0 / math.sqrt(NBR))).astype(bf16)
        return carry

    lax.fori_loop(0, 8, one_octant, 0)

    invariant = jnp.dot(msg[0], mix[0], preferred_element_type=f32)
    power = jnp.zeros((ATOMS, 128), f32)
    for lm in range(4, 9):
        tensor = jnp.dot(msg[lm], mix[2], preferred_element_type=f32)
        power = power + tensor * tensor
    invariant = invariant + power
    gating = jax.nn.sigmoid(invariant)
    node_out[...] = (state[...].astype(f32) + invariant * gating).astype(bf16)
    gate = gating * fw[...]
    lane_a = lax.broadcasted_iota(jnp.int32, (ATOMS, 128), 1)
    pushes = []
    for k in range(3):
        vector = jnp.dot(msg[1 + k], mix[1], preferred_element_type=f32)
        pushes.append(jnp.sum(vector * gate, axis=1, keepdims=True))
    force_out[...] = grads[...] + jnp.where(
        lane_a == 0, pushes[0], jnp.where(lane_a == 1, pushes[1], pushes[2])
    )


def short_call(shift, hs, hp, state, cols, codes, rw, mix, fw, grads):
    vmem_spec = pl.BlockSpec(memory_space=pltpu.VMEM)
    return pl.pallas_call(
        short_kernel,
        out_shape=(
            jax.ShapeDtypeStruct((ATOMS, 128), bf16),
            jax.ShapeDtypeStruct((ATOMS, 128), f32),
        ),
        in_specs=[pl.BlockSpec(memory_space=pltpu.SMEM)] + [vmem_spec] * 9,
        out_specs=(vmem_spec, vmem_spec),
        scratch_shapes=[
            pltpu.VMEM((1024, 128), bf16),
            pltpu.VMEM((OCT * 8, 128), f32),
            pltpu.VMEM((9 * 256, 1024), bf16),
            pltpu.VMEM((9, ATOMS, 128), bf16),
            pltpu.VMEM((9, OCT, 128), f32),
            pltpu.VMEM((64, 896), bf16),
            pltpu.VMEM((128, 896), bf16),
        ],
        compiler_params=pltpu.CompilerParams(vmem_limit_bytes=40 * 1024 * 1024),
        name="short_forces",
    )(shift, hs, hp, state, cols, codes, rw, mix, fw, grads)


def shards(tables, node_state, mesh_base, mesh_frac, charge, nbr_code, nbr_count,
           radial_weight, mix_weight, force_weight):
    index = jnp.stack([lax.axis_index("dx"), lax.axis_index("dy"), lax.axis_index("dz")])
    places = mesh_base.astype(f32) + mesh_frac
    local_base = (mesh_base.reshape(3, ATOMS) - index[:, None] * MB).astype(f32)
    rows = jnp.concatenate(
        [
            local_base,
            mesh_frac.reshape(3, ATOMS),
            charge.reshape(1, ATOMS),
            places.reshape(3, ATOMS),
            nbr_count.reshape(1, ATOMS).astype(f32),
            jnp.zeros((5, ATOMS), f32),
        ],
        axis=0,
    )
    cols = jnp.transpose(rows)
    pos = jnp.moveaxis(places, 0, 3)
    pos = jnp.pad(jnp.tile(pos, (1, 1, 1, 1, 4)), ((0, 0), (0, 0), (0, 0), (0, 5), (0, 0)))
    hs, hp, grads = mesh_call(node_state, pos, cols, tables)
    reach = 2 * index[:, None] + jnp.arange(4, dtype=jnp.int32)[None, :] - 1
    shift = jnp.where(reach < 0, -256.0, jnp.where(reach > 15, 256.0, 0.0)).astype(f32)
    node_next, forces = short_call(
        shift, hs, hp, node_state.reshape(ATOMS, 128), cols, nbr_code.reshape(ATOMS, NBR),
        radial_weight, mix_weight, force_weight.reshape(1, 128), grads,
    )
    forces = jnp.transpose(forces[:, :3]).reshape(3, 2, 2, 2, OCT)
    return (node_next.reshape(node_state.shape), forces)


def solution(mesh):
    placed = (
        P("dx", "dy", "dz", None, None),
        P(None, "dx", "dy", "dz", None),
        P(None, "dx", "dy", "dz", None),
        P("dx", "dy", "dz", None),
        P("dx", "dy", "dz", None, None),
        P("dx", "dy", "dz", None),
        P(),
        P(),
        P(),
    )
    tables = wave_tables()

    def run(*args):
        return shards(tuple(jnp.asarray(t) for t in tables), *args)

    return jax.shard_map(
        run,
        mesh=mesh,
        in_specs=placed,
        out_specs=(P("dx", "dy", "dz", None, None), P(None, "dx", "dy", "dz", None)),
        check_vma=False,
    )
```

```python
import functools
import math

import jax
import jax.numpy as jnp
import numpy as np
from jax import lax
from jax.experimental import pallas as pl
from jax.experimental.pallas import tpu as pltpu
from jax.sharding import PartitionSpec as P

NB = 8
NBR = 128
MB = 32
KZW = 8
OCT = 32
ATOMS = 8 * OCT
WIN = 40
EXT = 256

cell_size = 1.13
ewald_beta = 0.625
coulomb = 332.0637
sigma_low = 8.0
sigma_rate = 1.5
highest = lax.Precision.HIGHEST
MESH = pl.DeviceIdType.MESH
f32 = jnp.float32
bf16 = jnp.bfloat16


def wave_tables():
    cells = np.arange(WIN)
    angle = 2.0 * np.pi / EXT
    table_z = np.zeros((8, WIN, KZW, 2, 64))
    table_y = np.zeros((8, 2, 64, 8, 2, 64))
    back_x = np.zeros((8, 2, WIN, EXT))
    modes = np.arange(EXT)
    for d in range(8):
        at = d * MB + cells
        turn = angle * np.mod(at[:, None] * (1 + np.arange(KZW))[None, :], EXT)
        table_z[d, :, :, 0] = np.cos(turn)[:, :, None]
        table_z[d, :, :, 1] = -np.sin(turn)[:, :, None]
        turn = (angle * np.mod(at[:, None] * modes[None, :], EXT)).reshape(WIN, 8, 32)
        table_y[d, 0, :WIN, :, 0, :32] = np.cos(turn)
        table_y[d, 0, :WIN, :, 1, :32] = -np.sin(turn)
        table_y[d, 1, :WIN, :, 0, :32] = np.sin(turn)
        table_y[d, 1, :WIN, :, 1, :32] = np.cos(turn)
        turn = angle * np.mod(at[:, None] * modes[None, :], EXT)
        back_x[d, 0] = np.cos(turn)
        back_x[d, 1] = np.sin(turn)
    turn = angle * np.mod(modes[:, None] * modes[None, :], EXT)
    fore_x = np.stack([np.cos(turn), np.sin(turn)])
    return (
        table_z.reshape(8, WIN, KZW * 128).astype(np.float32),
        table_y.reshape(8, 128, 1024).astype(np.float32),
        fore_x.astype(np.float32),
        back_x.astype(np.float32),
    )


def dot_full(a, b):
    return jnp.dot(a, b, precision=highest, preferred_element_type=f32)


def spline_tables(base, frac, cell):
    left = 1.0 - frac
    square = frac * frac
    cube = square * frac
    weights = (
        left * left * left / 6.0,
        (3.0 * cube - 6.0 * square + 4.0) / 6.0,
        (-3.0 * cube + 3.0 * square + 3.0 * frac + 1.0) / 6.0,
        cube / 6.0,
    )
    slopes = (
        -0.5 * left * left,
        1.5 * square - 2.0 * frac,
        -1.5 * square + frac + 0.5,
        0.5 * square,
    )
    offset = cell - base
    table = jnp.zeros_like(offset)
    slope = jnp.zeros_like(offset)
    for t in range(4):
        hit = offset == float(t)
        table = jnp.where(hit, weights[t], table)
        slope = jnp.where(hit, slopes[t], slope)
    return table, slope


def top_power(count):
    power = count
    for bit in range(1, 8):
        power = jnp.where(count >= 2.0**bit, 2.0**bit, power)
    return power


def lane_of(quantity):
    return 8 * quantity


def gather_columns(base, frac, charge, count, anchor, rows, cols, posbuf):
    rows[...] = jnp.zeros_like(rows)
    for d in range(3):
        for cx in range(2):
            for cy in range(2):
                at = cx * 4 + cy * 2
                cells = base[d, cx, cy]
                part = frac[d, cx, cy]
                rows[d * 8 + at : d * 8 + at + 2, 0:OCT] = (cells - anchor[d]).astype(f32)
                rows[(3 + d) * 8 + at : (3 + d) * 8 + at + 2, 0:OCT] = part
                rows[(7 + d) * 8 + at : (7 + d) * 8 + at + 2, 0:OCT] = cells.astype(f32) + part
    for cx in range(2):
        for cy in range(2):
            at = cx * 4 + cy * 2
            rows[48 + at : 50 + at, 0:OCT] = charge[cx, cy]
            rows[80 + at : 82 + at, 0:OCT] = count[cx, cy].astype(f32)
    turned = jnp.transpose(rows[...])[0:OCT]
    for o in range(8):
        cols[o * OCT : (o + 1) * OCT] = pltpu.roll(turned, (128 - o) % 128, 1) if o else turned
        place = jnp.concatenate(
            [rows[(7 + d) * 8 + o : (7 + d) * 8 + o + 1] for d in range(3)] + [jnp.zeros((5, 128), f32)],
            axis=0,
        )
        place = place + pltpu.roll(place, 32, 1)
        posbuf[o // 4, o // 2 % 2, o % 2] = place + pltpu.roll(place, 64, 1)


def count_pairs(codes, cols, hist, first, last):
    sub8 = lax.broadcasted_iota(jnp.int32, (8, 128), 0)
    sub128 = lax.broadcasted_iota(jnp.int32, (128, 128), 0)
    slot = lax.broadcasted_iota(jnp.int32, (1, 128), 1).astype(f32)

    def count(g, c):
        for u in range(8):
            i = g * 8 + u
            row = codes[pl.ds(i, 1), :]
            live = slot < cols[pl.ds(i, 1), lane_of(10) : lane_of(10) + 1]
            row = jnp.where(live, row, 1023)
            high = jnp.broadcast_to(row >> 7, (8, 128))
            low = jnp.broadcast_to(row & 127, (128, 128))
            a = jnp.where(high == sub8, 1.0, 0.0).astype(bf16)
            b = jnp.where(low == sub128, 1.0, 0.0).astype(bf16)
            hist[pl.ds(pl.multiple_of(i * 8, 8), 8), :] = lax.dot_general(
                a, b, (((1,), (1,)), ((), ())), preferred_element_type=f32
            )
        return c

    lax.fori_loop(first * 4, last * 4, count, 0)


def line_up(octant, hs, cand):
    cx, cy, cz = octant // 4, octant // 2 % 2, octant % 2
    for side in range(27):
        hx, hy, hz = cx + side // 9, cy + side // 3 % 3, cz + side % 3
        cand[side * 32 : side * 32 + 32] = hs[hx, hy, hz]
    cand[864:896] = jnp.zeros((32, 128), bf16)


def line_up_places(octant, hp, near, index):
    cx, cy, cz = octant // 4, octant // 2 % 2, octant % 2
    lane = lax.broadcasted_iota(jnp.int32, (8, 128), 1)
    sub8 = lax.broadcasted_iota(jnp.int32, (8, 128), 0)

    def wrap(here, h):
        reach = 2 * here + h - 1
        return jnp.where(reach < 0, -float(EXT), jnp.where(reach > 15, float(EXT), 0.0)).astype(f32)

    wrap_x = [wrap(index[0], cx + n) for n in range(3)]
    wrap_y = [wrap(index[1], cy + n) for n in range(3)]
    wrap_z = [wrap(index[2], cz + n) for n in range(3)]
    tiles = []
    for side in range(27):
        nx, ny, nz = side // 9, side // 3 % 3, side % 3
        shift = jnp.where(sub8 == 0, wrap_x[nx], jnp.where(sub8 == 1, wrap_y[ny], wrap_z[nz]))
        tiles.append(hp[cx + nx, cy + ny, cz + nz] + shift)
    tiles.append(tiles[26])
    for t in range(7):
        four = tiles[4 * t : 4 * t + 4]
        near[octant, t] = jnp.where(
            lane < 32, four[0], jnp.where(lane < 64, four[1], jnp.where(lane < 96, four[2], four[3]))
        )


def edge_pass(octant, cols, near, hist, rw, cand, lhs, extra, pick, sums_out):
    sub8 = lax.broadcasted_iota(jnp.int32, (8, 128), 0)
    sub128 = lax.broadcasted_iota(jnp.int32, (128, 128), 0)
    lane128 = lax.broadcasted_iota(jnp.int32, (128, 128), 1)
    lane32 = lax.broadcasted_iota(jnp.int32, (OCT, 128), 1)
    before = jnp.where(sub128 < lane128, 1.0, 0.0).astype(bf16)
    ones = jnp.ones((128, 128), bf16)
    place_id = (sub128 & 63).astype(f32)
    root3, root5, root15 = math.sqrt(3.0), math.sqrt(5.0), math.sqrt(15.0)
    rates = [
        -(cell_size**2) / (sigma_low * sigma_rate**b) ** 2 / math.log(2.0) for b in range(NB)
    ]
    row0 = pl.multiple_of(octant * OCT, OCT)
    hist0 = octant * 256

    def listed(t):
        return hist[pl.ds(hist0 + t, OCT, 8), :]

    flags = jnp.zeros((8, 128), f32)
    for t in range(7):
        at = slice(t * 128, (t + 1) * 128)
        place = near[octant, t]
        first = place.astype(bf16).astype(f32)
        rest = place - first
        second = rest.astype(bf16).astype(f32)
        extra[32:48, at] = jnp.concatenate([first, second], axis=0).astype(bf16)
        extra[48:64, at] = jnp.concatenate([rest - second, jnp.zeros_like(rest)], axis=0).astype(bf16)
        over = jnp.maximum(listed(t) - 2.0, 0.0)
        extra[0:OCT, at] = over.astype(bf16)
        flag = jnp.where(jnp.max(over, axis=0, keepdims=True) > 0.0, 1.0, 0.0)
        flags = jnp.where(sub8 == t, flag, flags)
    flags_b = flags.astype(bf16)
    rank = jnp.dot(flags_b, before, preferred_element_type=f32)
    sums = jnp.dot(flags_b, ones, preferred_element_type=f32)
    offset = jnp.zeros((1, 128), f32)
    for t in range(7):
        key = jnp.where(flags[t : t + 1] > 0.0, rank[t : t + 1] + offset, -1.0)
        pick[:, t * 128 : (t + 1) * 128] = jnp.where(key == place_id, 1.0, 0.0).astype(bf16)
        offset = offset + sums[t : t + 1]
    picked = lax.dot_general(
        extra[...], pick[...], (((1,), (1,)), ((), ())), preferred_element_type=f32
    )
    cand[896:1024] = jnp.dot(pick[...], cand[0:896], preferred_element_type=f32).astype(bf16)
    more = picked[0:OCT]
    power = top_power(more)
    second = top_power(more - power)
    left = jnp.max(jnp.maximum(more - power - second, offset - 64.0), axis=0, keepdims=True)
    left = jnp.max(left, axis=1, keepdims=True)
    spare = jnp.where(left > 0.0, 0.0, jnp.where(lane32 < 64, power, second))
    spare_place = picked[32:40] + picked[40:48] + picked[48:56]
    own = [
        jnp.broadcast_to(cols[pl.ds(row0, OCT), lane_of(7 + d) : lane_of(7 + d) + 1], (OCT, 128))
        for d in range(3)
    ]
    for t in range(8):
        place = spare_place if t == 7 else near[octant, t]
        times_all = spare if t == 7 else jnp.minimum(listed(t), 2.0)
        for h in range(2):
            rows = slice(16 * h, 16 * h + 16)
            delta = [place[d : d + 1] - own[d][rows] for d in range(3)]
            square = delta[0] * delta[0] + delta[1] * delta[1] + delta[2] * delta[2]
            inv = lax.rsqrt(square + 1.0)
            ux, uy, uz = (d * inv for d in delta)
            times = times_all[rows]
            radial = [jnp.exp2(square * rates[b]) * times for b in range(NB)]
            angular = [
                None,
                root3 * ux,
                root3 * uy,
                root3 * uz,
                root15 * ux * uy,
                root15 * uy * uz,
                0.5 * root5 * (3.0 * uz * uz - 1.0),
                root15 * ux * uz,
                0.5 * root15 * (ux * ux - uy * uy),
            ]
            for lm in range(9):
                for b in range(NB):
                    value = radial[b] if lm == 0 else radial[b] * angular[lm]
                    at = (lm * NB + b) * OCT + 16 * h
                    lhs[at : at + 16, t * 128 : (t + 1) * 128] = value.astype(bf16)
    for lm in range(9):
        summed = jnp.dot(lhs[lm * 256 : (lm + 1) * 256], cand[...], preferred_element_type=f32)
        message = summed[0:OCT] * rw[0:1]
        for b in range(1, NB):
            message = message + summed[b * OCT : (b + 1) * OCT] * rw[b : b + 1]
        sums_out(lm, message)
    return left


def mesh_kernel(
    state, base, frac, charge, count, codes_all, rw, tz_all, ty_all, fx_all, bx_all,
    hs, grads, near, hist, total, cols, lefts,
    hp, posbuf, rows, codes, tz, ty, fx, bx, wz, dwz, xt, yt, ys,
    s1, r1, s2, r2, s3, r3, s4, r4, s5, r5, grid, cand, lhs, extra, pick,
    send_sem, recv_sem, hsend, hrecv, lsem,
):
    ix, iy, iz = lax.axis_index("dx"), lax.axis_index("dy"), lax.axis_index("dz")
    here = {"dx": ix, "dy": iy, "dz": iz}
    barrier = pltpu.get_barrier_semaphore()

    for axis in ("dx", "dy", "dz"):

        def greet(s, carry, axis=axis):
            pl.semaphore_signal(
                barrier, inc=1, device_id={axis: lax.rem(here[axis] + s, 8)}, device_id_type=MESH
            )
            return carry

        lax.fori_loop(1, 8, greet, 0)

    local = [
        pltpu.make_async_copy(tz_all.at[iz], tz, lsem.at[0]),
        pltpu.make_async_copy(ty_all.at[iy], ty, lsem.at[1]),
        pltpu.make_async_copy(bx_all.at[ix], bx, lsem.at[2]),
        pltpu.make_async_copy(state, hs.at[pl.ds(1, 2), pl.ds(1, 2), pl.ds(1, 2)], lsem.at[3]),
        pltpu.make_async_copy(fx_all, fx, lsem.at[4]),
        pltpu.make_async_copy(codes_all, codes, lsem.at[5]),
    ]
    for copy in local:
        copy.start()

    gather_columns(base, frac, charge, count, (ix * MB, iy * MB, iz * MB), rows, cols, posbuf)
    hp[1:3, 1:3, 1:3] = posbuf[...]
    lane = lax.broadcasted_iota(jnp.int32, (ATOMS, 128), 1)
    cell = lane.astype(f32)
    half_cell = (lane % 64).astype(f32)

    def column(c):
        return jnp.broadcast_to(cols[:, lane_of(c) : lane_of(c) + 1], (ATOMS, 128))

    table, slope = spline_tables(column(2), column(5), cell)
    local[0].wait()
    wz[...] = dot_full(table[:, :WIN], tz[...])
    dwz[:, 0:128] = slope
    table, slope = spline_tables(column(1), column(4), half_cell)
    yt[...] = table
    ys[...] = slope
    table, slope = spline_tables(column(0), column(3), cell)
    xt[0:ATOMS] = table
    xt[ATOMS : 2 * ATOMS] = slope
    left = jnp.transpose(table * column(6))[:WIN]
    for k in range(KZW):
        s1[k] = dot_full(left, yt[...] * wz[:, k * 128 : (k + 1) * 128])

    pl.semaphore_wait(barrier, 21)

    def halo(stage, axis, src_up, dst_up, src_down, dst_down):
        out = []
        for which in range(2):
            full = (hs, hp)[which]
            first = (state, posbuf)[which]
            up_src = first.at[src_up] if stage == 0 else full.at[src_up]
            down_src = first.at[src_down] if stage == 0 else full.at[src_down]
            for way, (src, dst, step) in enumerate(
                ((up_src, full.at[dst_up], 1), (down_src, full.at[dst_down], 7))
            ):
                n = stage * 4 + which * 2 + way
                out.append(
                    pltpu.make_async_remote_copy(
                        src_ref=src,
                        dst_ref=dst,
                        send_sem=hsend.at[n],
                        recv_sem=hrecv.at[n],
                        device_id={axis: lax.rem(here[axis] + step, 8)},
                        device_id_type=MESH,
                    )
                )
        return out

    mid = pl.ds(1, 2)
    full = pl.ds(0, 4)

    def one(n):
        return pl.ds(n, 1)

    halo_x = halo(0, "dx", (one(1),), (one(0), mid, mid), (one(0),), (one(3), mid, mid))
    halo_y = halo(
        1, "dy", (full, one(2), mid), (full, one(0), mid), (full, one(1), mid), (full, one(3), mid)
    )
    halo_z = halo(
        2, "dz", (full, full, one(2)), (full, full, one(0)), (full, full, one(1)), (full, full, one(3))
    )

    def link(phase, axis, s, src, dst):
        return pltpu.make_async_remote_copy(
            src_ref=src,
            dst_ref=dst,
            send_sem=send_sem.at[phase, s],
            recv_sem=recv_sem.at[phase, s],
            device_id={axis: lax.rem(here[axis] + s, 8)},
            device_id_type=MESH,
        )

    def deal(phase, axis, s, sent, got):
        return link(phase, axis, s, sent.at[lax.rem(here[axis] + s, 8)], got.at[s])

    def share(phase, axis, s, sent, got, arriving):
        slot = lax.rem(here[axis] + 8 - s, 8) if arriving else here[axis]
        return link(phase, axis, s, sent, got.at[slot])

    def start_deal(phase, axis, sent, got):
        def body(s, carry):
            deal(phase, axis, s, sent, got).start()
            return carry

        lax.fori_loop(1, 8, body, 0)

    def wait_deal(phase, axis, sent, got):
        def body(s, carry):
            deal(phase, axis, s, sent, got).wait()
            return carry

        lax.fori_loop(1, 8, body, 0)
        total = sent[here[axis]]
        for s in range(1, 8):
            total = total + got[s]
        return total

    def start_share(phase, axis, sent, got):
        got[here[axis]] = sent[...]

        def body(s, carry):
            share(phase, axis, s, sent, got, False).start()
            return carry

        lax.fori_loop(1, 8, body, 0)

    def wait_share(phase, axis, sent, got):
        def body(s, carry):
            share(phase, axis, s, sent, got, True).wait()
            return carry

        lax.fori_loop(1, 8, body, 0)

    start_deal(0, "dz", s1, r1)
    for copy in halo_x:
        copy.start()
    local[1].wait()
    local[3].wait()
    local[5].wait()
    count_pairs(codes, cols, hist, 0, 3)
    for copy in halo_x:
        copy.wait()
    for copy in halo_y:
        copy.start()
    spread = dot_full(wait_deal(0, "dz", s1, r1), ty[...])
    for p in range(8):
        s2[p] = spread[:, p * 128 : (p + 1) * 128]
    start_deal(1, "dy", s2, r2)
    count_pairs(codes, cols, hist, 3, 6)
    for copy in halo_y:
        copy.wait()
    for copy in halo_z:
        copy.start()

    kx = lax.broadcasted_iota(jnp.int32, (EXT, 128), 0)
    lane_k = lax.broadcasted_iota(jnp.int32, (EXT, 128), 1)
    ky = iy * 32 + (lane_k % 64) % 32

    def folded(k):
        return jnp.where(2 * k >= EXT, k - EXT, k).astype(f32) / (cell_size * EXT)

    wave_z = (iz + 1).astype(f32) / (cell_size * EXT)
    wave_square = folded(kx) * folded(kx) + folded(ky) * folded(ky) + wave_z * wave_z
    volume = cell_size**3 * EXT * EXT * EXT
    green = (
        coulomb
        / (math.pi * volume)
        * jnp.exp(-(math.pi**2) / ewald_beta**2 * wave_square)
        / wave_square
    )
    sign = jnp.where(lane_k < 64, 1.0, -1.0).astype(f32)

    s3[...] = wait_deal(1, "dy", s2, r2)
    start_share(2, "dx", s3, r3)
    count_pairs(codes, cols, hist, 6, 8)
    dwz[...] = dot_full(dwz[:, 0:WIN], tz[...])
    local[2].wait()
    local[4].wait()
    wait_share(2, "dx", s3, r3)
    for d in range(8):
        grid[d * 32 : d * 32 + 8] = r3[d, 0:8] + r3[(d + 7) % 8, 32:40]
        grid[d * 32 + 8 : d * 32 + 32] = r3[d, 8:32]
    lined = grid[...]
    spec = dot_full(fx[0], lined) + dot_full(fx[1], sign * pltpu.roll(lined, 64, 1))
    scaled = spec * green
    s4[...] = dot_full(bx[0], scaled) - dot_full(bx[1], sign * pltpu.roll(scaled, 64, 1))
    start_share(3, "dy", s4, r4)
    for copy in halo_z:
        copy.wait()

    def edges(octant, carry):
        line_up(octant, hs, cand)
        line_up_places(octant, hp, near, (ix, iy, iz))

        def keep(lm, message):
            total[lm, pl.ds(pl.multiple_of(octant * OCT, OCT), OCT), :] = message

        left = edge_pass(octant, cols, near, hist, rw, cand, lhs, extra, pick, keep)
        lefts[pl.ds(octant, 1), :] = jnp.broadcast_to(left, (1, 128))
        return carry

    lax.fori_loop(0, 2, edges, 0)
    wait_share(3, "dy", s4, r4)
    back = jnp.zeros((WIN, 128), f32)
    for p in range(8):
        back = back + lax.dot_general(
            r4[p],
            ty[:, p * 128 : (p + 1) * 128],
            (((1,), (1,)), ((), ())),
            precision=highest,
            preferred_element_type=f32,
        )
    s5[...] = back
    start_share(4, "dz", s5, r5)
    lax.fori_loop(2, 8, edges, 0)
    wait_share(4, "dz", s5, r5)
    along = jnp.zeros((ATOMS, 128), f32)
    along_z = jnp.zeros((ATOMS, 128), f32)
    tilted = jnp.zeros((ATOMS, 128), f32)
    for k in range(KZW):
        near = dot_full(xt[:, :WIN], r5[k])
        wave = wz[:, k * 128 : (k + 1) * 128]
        along = along + near[:ATOMS] * wave
        along_z = along_z + near[:ATOMS] * dwz[:, k * 128 : (k + 1) * 128]
        tilted = tilted + near[ATOMS:] * wave
    grad_x = jnp.sum(tilted * yt[...], axis=1, keepdims=True)
    grad_y = jnp.sum(along * ys[...], axis=1, keepdims=True)
    grad_z = jnp.sum(along_z * yt[...], axis=1, keepdims=True)
    scale = -(column(6) / cell_size) * 2.0
    grads[...] = scale * jnp.where(lane == 0, grad_x, jnp.where(lane == 1, grad_y, grad_z))


def mesh_call(state, base, frac, charge, count, codes, rw, tables):
    hbm_spec = pl.BlockSpec(memory_space=pltpu.HBM)
    vmem_spec = pl.BlockSpec(memory_space=pltpu.VMEM)
    block = (8, WIN, 128)
    return pl.pallas_call(
        mesh_kernel,
        out_shape=(
            jax.ShapeDtypeStruct((4, 4, 4, OCT, 128), bf16),
            jax.ShapeDtypeStruct((ATOMS, 128), f32),
            jax.ShapeDtypeStruct((8, 7, 8, 128), f32),
            jax.ShapeDtypeStruct((ATOMS * 8, 128), f32),
            jax.ShapeDtypeStruct((9, ATOMS, 128), f32),
            jax.ShapeDtypeStruct((ATOMS, 128), f32),
            jax.ShapeDtypeStruct((8, 128), f32),
        ),
        in_specs=[hbm_spec] + [vmem_spec] * 4 + [hbm_spec, vmem_spec] + [hbm_spec] * 4,
        out_specs=(vmem_spec,) * 7,
        scratch_shapes=[
            pltpu.VMEM((4, 4, 4, 8, 128), f32),
            pltpu.VMEM((2, 2, 2, 8, 128), f32),
            pltpu.VMEM((128, 128), f32),
            pltpu.VMEM((ATOMS, 128), jnp.int32),
            pltpu.VMEM((WIN, 1024), f32),
            pltpu.VMEM((128, 1024), f32),
            pltpu.VMEM((2, EXT, EXT), f32),
            pltpu.VMEM((2, WIN, EXT), f32),
            pltpu.VMEM((ATOMS, 1024), f32),
            pltpu.VMEM((ATOMS, 1024), f32),
            pltpu.VMEM((2 * ATOMS, 128), f32),
            pltpu.VMEM((ATOMS, 128), f32),
            pltpu.VMEM((ATOMS, 128), f32),
            pltpu.VMEM(block, f32),
            pltpu.VMEM(block, f32),
            pltpu.VMEM(block, f32),
            pltpu.VMEM(block, f32),
            pltpu.VMEM((WIN, 128), f32),
            pltpu.VMEM(block, f32),
            pltpu.VMEM((WIN, 128), f32),
            pltpu.VMEM(block, f32),
            pltpu.VMEM((WIN, 128), f32),
            pltpu.VMEM(block, f32),
            pltpu.VMEM((EXT, 128), f32),
            pltpu.VMEM((1024, 128), bf16),
            pltpu.VMEM((9 * 256, 1024), bf16),
            pltpu.VMEM((64, 896), bf16),
            pltpu.VMEM((128, 896), bf16),
            pltpu.SemaphoreType.DMA((5, 8)),
            pltpu.SemaphoreType.DMA((5, 8)),
            pltpu.SemaphoreType.DMA((12,)),
            pltpu.SemaphoreType.DMA((12,)),
            pltpu.SemaphoreType.DMA((6,)),
        ],
        compiler_params=pltpu.CompilerParams(
            collective_id=0, has_side_effects=True, vmem_limit_bytes=60 * 1024 * 1024
        ),
        name="mesh_forces",
    )(state, base, frac, charge, count, codes, rw, *tables)


def node_kernel(
    hs_in, near_in, hist_in, state, total_in, cols, lefts, rw, mix, fw, grads,
    node_out, force_out,
    cand, lhs, extra, pick, hs, near, hist, total, sem,
):
    def finish(octant, carry):
        rows = pl.ds(pl.multiple_of(octant * OCT, OCT), OCT)
        hist_rows = pl.ds(pl.multiple_of(octant * 256, 256), 256)

        @pl.when(jnp.max(lefts[pl.ds(octant, 1), :]) > 0.0)
        def _():
            line_up(octant, hs, cand)

            def add(lm, message):
                total[lm, rows, :] = total[lm, rows, :] + message

            def one_pass(again):
                hist[hist_rows, :] = jnp.maximum(hist[hist_rows, :] - 2.0, 0.0)
                left = edge_pass(octant, cols, near, hist, rw, cand, lhs, extra, pick, add)
                return jnp.max(left) > 0.0

            lax.while_loop(lambda again: again, one_pass, jnp.bool_(True))

        return carry

    total[...] = total_in[...]

    @pl.when(jnp.max(lefts[...]) > 0.0)
    def _():
        for n, (source, target) in enumerate(((hs_in, hs), (near_in, near), (hist_in, hist))):
            copy = pltpu.make_async_copy(source, target, sem.at[n])
            copy.start()
            copy.wait()
        lax.fori_loop(0, 8, finish, 0)

    def message(lm):
        return (total[lm] * (1.0 / math.sqrt(NBR))).astype(bf16)

    invariant = jnp.dot(message(0), mix[0], preferred_element_type=f32)
    power = jnp.zeros((ATOMS, 128), f32)
    for lm in range(4, 9):
        tensor = jnp.dot(message(lm), mix[2], preferred_element_type=f32)
        power = power + tensor * tensor
    invariant = invariant + power
    gating = jax.nn.sigmoid(invariant)
    node_out[...] = (state[...].astype(f32) + invariant * gating).astype(bf16)
    gate = gating * fw[...]
    lane = lax.broadcasted_iota(jnp.int32, (OCT, 128), 1)
    lined = jnp.zeros((OCT, 128), f32)
    for k in range(3):
        vector = jnp.dot(message(1 + k), mix[1], preferred_element_type=f32)
        push = jnp.sum(vector * gate, axis=1, keepdims=True) + grads[:, k : k + 1]
        for o in range(8):
            lined = jnp.where(lane == k * 8 + o, push[o * OCT : (o + 1) * OCT], lined)
    turned = jnp.transpose(jnp.concatenate([lined, jnp.zeros((96, 128), f32)], axis=0))
    for k in range(3):
        for cx in range(2):
            for cy in range(2):
                at = k * 8 + cx * 4 + cy * 2
                force_out[k, cx, cy] = turned[at : at + 2, 0:OCT]


def node_call(hs, near, hist, state, total, cols, lefts, rw, mix, fw, grads):
    vmem_spec = pl.BlockSpec(memory_space=pltpu.VMEM)
    return pl.pallas_call(
        node_kernel,
        out_shape=(
            jax.ShapeDtypeStruct((ATOMS, 128), bf16),
            jax.ShapeDtypeStruct((3, 2, 2, 2, OCT), f32),
        ),
        in_specs=[pl.BlockSpec(memory_space=pltpu.HBM)] * 3 + [vmem_spec] * 8,
        out_specs=(vmem_spec, vmem_spec),
        scratch_shapes=[
            pltpu.VMEM((1024, 128), bf16),
            pltpu.VMEM((9 * 256, 1024), bf16),
            pltpu.VMEM((64, 896), bf16),
            pltpu.VMEM((128, 896), bf16),
            pltpu.VMEM((4, 4, 4, OCT, 128), bf16),
            pltpu.VMEM((8, 7, 8, 128), f32),
            pltpu.VMEM((ATOMS * 8, 128), f32),
            pltpu.VMEM((9, ATOMS, 128), f32),
            pltpu.SemaphoreType.DMA((3,)),
        ],
        compiler_params=pltpu.CompilerParams(vmem_limit_bytes=60 * 1024 * 1024),
        name="node_update",
    )(hs, near, hist, state, total, cols, lefts, rw, mix, fw, grads)


def shards(tables, node_state, mesh_base, mesh_frac, charge, nbr_code, nbr_count,
           radial_weight, mix_weight, force_weight):
    hs, grads, near, hist, total, cols, lefts = mesh_call(
        node_state, mesh_base, mesh_frac, charge, nbr_count,
        nbr_code.reshape(ATOMS, NBR), radial_weight, tables,
    )
    node_next, forces = node_call(
        hs, near, hist, node_state.reshape(ATOMS, 128), total, cols, lefts, radial_weight, mix_weight,
        force_weight.reshape(1, 128), grads,
    )
    return (node_next.reshape(node_state.shape), forces)


def solution(mesh):
    placed = (
        P("dx", "dy", "dz", None, None),
        P(None, "dx", "dy", "dz", None),
        P(None, "dx", "dy", "dz", None),
        P("dx", "dy", "dz", None),
        P("dx", "dy", "dz", None, None),
        P("dx", "dy", "dz", None),
        P(),
        P(),
        P(),
    )
    tables = wave_tables()

    def run(*args):
        return shards(tuple(jnp.asarray(t) for t in tables), *args)

    return jax.shard_map(
        run,
        mesh=mesh,
        in_specs=placed,
        out_specs=(P("dx", "dy", "dz", None, None), P(None, "dx", "dy", "dz", None)),
        check_vma=False,
    )
```

```python
import functools
import math

import jax
import jax.numpy as jnp
import numpy as np
from jax import lax
from jax.experimental import pallas as pl
from jax.experimental.pallas import tpu as pltpu
from jax.sharding import PartitionSpec as P

NB = 8
NBR = 128
MB = 32
KZW = 8
OCT = 32
ATOMS = 8 * OCT
WIN = 40
EXT = 256

cell_size = 1.13
ewald_beta = 0.625
coulomb = 332.0637
sigma_low = 8.0
sigma_rate = 1.5
highest = lax.Precision.HIGHEST
MESH = pl.DeviceIdType.MESH
f32 = jnp.float32
bf16 = jnp.bfloat16


def wave_tables():
    cells = np.arange(WIN)
    angle = 2.0 * np.pi / EXT
    table_z = np.zeros((8, WIN, KZW, 2, 64))
    table_y = np.zeros((8, 2, 64, 8, 2, 64))
    back_x = np.zeros((8, 2, WIN, EXT))
    modes = np.arange(EXT)
    for d in range(8):
        at = d * MB + cells
        turn = angle * np.mod(at[:, None] * (1 + np.arange(KZW))[None, :], EXT)
        table_z[d, :, :, 0] = np.cos(turn)[:, :, None]
        table_z[d, :, :, 1] = -np.sin(turn)[:, :, None]
        turn = (angle * np.mod(at[:, None] * modes[None, :], EXT)).reshape(WIN, 8, 32)
        table_y[d, 0, :WIN, :, 0, :32] = np.cos(turn)
        table_y[d, 0, :WIN, :, 1, :32] = -np.sin(turn)
        table_y[d, 1, :WIN, :, 0, :32] = np.sin(turn)
        table_y[d, 1, :WIN, :, 1, :32] = np.cos(turn)
        turn = angle * np.mod(at[:, None] * modes[None, :], EXT)
        back_x[d, 0] = np.cos(turn)
        back_x[d, 1] = np.sin(turn)
    turn = angle * np.mod(modes[:, None] * modes[None, :], EXT)
    fore_x = np.stack([np.cos(turn), np.sin(turn)])
    return (
        table_z.reshape(8, WIN, KZW * 128).astype(np.float32),
        table_y.reshape(8, 128, 1024).astype(np.float32),
        fore_x.astype(np.float32),
        back_x.astype(np.float32),
    )


def dot_full(a, b):
    return jnp.dot(a, b, precision=highest, preferred_element_type=f32)


def spline_tables(base, frac, cell):
    left = 1.0 - frac
    square = frac * frac
    cube = square * frac
    weights = (
        left * left * left / 6.0,
        (3.0 * cube - 6.0 * square + 4.0) / 6.0,
        (-3.0 * cube + 3.0 * square + 3.0 * frac + 1.0) / 6.0,
        cube / 6.0,
    )
    slopes = (
        -0.5 * left * left,
        1.5 * square - 2.0 * frac,
        -1.5 * square + frac + 0.5,
        0.5 * square,
    )
    offset = cell - base
    table = jnp.zeros_like(offset)
    slope = jnp.zeros_like(offset)
    for t in range(4):
        hit = offset == float(t)
        table = jnp.where(hit, weights[t], table)
        slope = jnp.where(hit, slopes[t], slope)
    return table, slope


def top_power(count):
    power = count
    for bit in range(1, 8):
        power = jnp.where(count >= 2.0**bit, 2.0**bit, power)
    return power


def lane_of(quantity):
    return 8 * quantity


def gather_columns(base, frac, charge, count, anchor, rows, cols, posbuf):
    rows[...] = jnp.zeros_like(rows)
    for d in range(3):
        for cx in range(2):
            for cy in range(2):
                at = cx * 4 + cy * 2
                cells = base[d, cx, cy]
                part = frac[d, cx, cy]
                rows[d * 8 + at : d * 8 + at + 2, 0:OCT] = (cells - anchor[d]).astype(f32)
                rows[(3 + d) * 8 + at : (3 + d) * 8 + at + 2, 0:OCT] = part
                rows[(7 + d) * 8 + at : (7 + d) * 8 + at + 2, 0:OCT] = cells.astype(f32) + part
    for cx in range(2):
        for cy in range(2):
            at = cx * 4 + cy * 2
            rows[48 + at : 50 + at, 0:OCT] = charge[cx, cy]
            rows[80 + at : 82 + at, 0:OCT] = count[cx, cy].astype(f32)
    turned = jnp.transpose(rows[...])[0:OCT]
    for o in range(8):
        cols[o * OCT : (o + 1) * OCT] = pltpu.roll(turned, (128 - o) % 128, 1) if o else turned
        place = jnp.concatenate(
            [rows[(7 + d) * 8 + o : (7 + d) * 8 + o + 1] for d in range(3)] + [jnp.zeros((5, 128), f32)],
            axis=0,
        )
        place = place + pltpu.roll(place, 32, 1)
        posbuf[o // 4, o // 2 % 2, o % 2] = place + pltpu.roll(place, 64, 1)


def count_pairs(codes, cols, hist, first, last):
    sub8 = lax.broadcasted_iota(jnp.int32, (8, 128), 0)
    sub128 = lax.broadcasted_iota(jnp.int32, (128, 128), 0)
    slot = lax.broadcasted_iota(jnp.int32, (1, 128), 1).astype(f32)

    def count(g, c):
        for u in range(8):
            i = g * 8 + u
            row = codes[pl.ds(i, 1), :]
            live = slot < cols[pl.ds(i, 1), lane_of(10) : lane_of(10) + 1]
            row = jnp.where(live, row, 1023)
            high = jnp.broadcast_to(row >> 7, (8, 128))
            low = jnp.broadcast_to(row & 127, (128, 128))
            a = jnp.where(high == sub8, 1.0, 0.0).astype(bf16)
            b = jnp.where(low == sub128, 1.0, 0.0).astype(bf16)
            hist[pl.ds(pl.multiple_of(i * 8, 8), 8), :] = lax.dot_general(
                a, b, (((1,), (1,)), ((), ())), preferred_element_type=f32
            )
        return c

    lax.fori_loop(first * 4, last * 4, count, 0)


def line_up(octant, hs, cand):
    cx, cy, cz = octant // 4, octant // 2 % 2, octant % 2
    for side in range(27):
        hx, hy, hz = cx + side // 9, cy + side // 3 % 3, cz + side % 3
        cand[side * 32 : side * 32 + 32] = hs[hx, hy, hz]
    cand[864:896] = jnp.zeros((32, 128), bf16)


def line_up_places(octant, hp, near, index):
    cx, cy, cz = octant // 4, octant // 2 % 2, octant % 2
    lane = lax.broadcasted_iota(jnp.int32, (8, 128), 1)
    sub8 = lax.broadcasted_iota(jnp.int32, (8, 128), 0)

    def wrap(here, h):
        reach = 2 * here + h - 1
        return jnp.where(reach < 0, -float(EXT), jnp.where(reach > 15, float(EXT), 0.0)).astype(f32)

    wrap_x = [wrap(index[0], cx + n) for n in range(3)]
    wrap_y = [wrap(index[1], cy + n) for n in range(3)]
    wrap_z = [wrap(index[2], cz + n) for n in range(3)]
    tiles = []
    for side in range(27):
        nx, ny, nz = side // 9, side // 3 % 3, side % 3
        shift = jnp.where(sub8 == 0, wrap_x[nx], jnp.where(sub8 == 1, wrap_y[ny], wrap_z[nz]))
        tiles.append(hp[cx + nx, cy + ny, cz + nz] + shift)
    tiles.append(tiles[26])
    for t in range(7):
        four = tiles[4 * t : 4 * t + 4]
        near[octant, t] = jnp.where(
            lane < 32, four[0], jnp.where(lane < 64, four[1], jnp.where(lane < 96, four[2], four[3]))
        )


def edge_pass(octant, cols, near, hist, rw, cand, lhs, extra, pick, sums_out):
    sub8 = lax.broadcasted_iota(jnp.int32, (8, 128), 0)
    sub128 = lax.broadcasted_iota(jnp.int32, (128, 128), 0)
    lane128 = lax.broadcasted_iota(jnp.int32, (128, 128), 1)
    lane32 = lax.broadcasted_iota(jnp.int32, (OCT, 128), 1)
    before = jnp.where(sub128 < lane128, 1.0, 0.0).astype(bf16)
    ones = jnp.ones((128, 128), bf16)
    place_id = (sub128 & 63).astype(f32)
    root3, root5, root15 = math.sqrt(3.0), math.sqrt(5.0), math.sqrt(15.0)
    rates = [
        -(cell_size**2) / (sigma_low * sigma_rate**b) ** 2 / math.log(2.0) for b in range(NB)
    ]
    row0 = pl.multiple_of(octant * OCT, OCT)
    hist0 = octant * 256

    def listed(t):
        return hist[pl.ds(hist0 + t, OCT, 8), :]

    flags = jnp.zeros((8, 128), f32)
    for t in range(7):
        at = slice(t * 128, (t + 1) * 128)
        place = near[octant, t]
        first = place.astype(bf16).astype(f32)
        rest = place - first
        second = rest.astype(bf16).astype(f32)
        extra[32:48, at] = jnp.concatenate([first, second], axis=0).astype(bf16)
        extra[48:64, at] = jnp.concatenate([rest - second, jnp.zeros_like(rest)], axis=0).astype(bf16)
        over = jnp.maximum(listed(t) - 2.0, 0.0)
        extra[0:OCT, at] = over.astype(bf16)
        flag = jnp.where(jnp.max(over, axis=0, keepdims=True) > 0.0, 1.0, 0.0)
        flags = jnp.where(sub8 == t, flag, flags)
    flags_b = flags.astype(bf16)
    rank = jnp.dot(flags_b, before, preferred_element_type=f32)
    sums = jnp.dot(flags_b, ones, preferred_element_type=f32)
    offset = jnp.zeros((1, 128), f32)
    for t in range(7):
        key = jnp.where(flags[t : t + 1] > 0.0, rank[t : t + 1] + offset, -1.0)
        pick[:, t * 128 : (t + 1) * 128] = jnp.where(key == place_id, 1.0, 0.0).astype(bf16)
        offset = offset + sums[t : t + 1]
    picked = lax.dot_general(
        extra[...], pick[...], (((1,), (1,)), ((), ())), preferred_element_type=f32
    )
    cand[896:1024] = jnp.dot(pick[...], cand[0:896], preferred_element_type=f32).astype(bf16)
    more = picked[0:OCT]
    power = top_power(more)
    second = top_power(more - power)
    left = jnp.max(jnp.maximum(more - power - second, offset - 64.0), axis=0, keepdims=True)
    left = jnp.max(left, axis=1, keepdims=True)
    spare = jnp.where(left > 0.0, 0.0, jnp.where(lane32 < 64, power, second))
    spare_place = picked[32:40] + picked[40:48] + picked[48:56]
    own = [
        jnp.broadcast_to(cols[pl.ds(row0, OCT), lane_of(7 + d) : lane_of(7 + d) + 1], (OCT, 128))
        for d in range(3)
    ]
    for t in range(8):
        place = spare_place if t == 7 else near[octant, t]
        times_all = spare if t == 7 else jnp.minimum(listed(t), 2.0)
        for h in range(2):
            rows = slice(16 * h, 16 * h + 16)
            delta = [place[d : d + 1] - own[d][rows] for d in range(3)]
            square = delta[0] * delta[0] + delta[1] * delta[1] + delta[2] * delta[2]
            inv = lax.rsqrt(square + 1.0)
            ux, uy, uz = (d * inv for d in delta)
            times = times_all[rows]
            radial = [jnp.exp2(square * rates[b]) * times for b in range(NB)]
            angular = [
                None,
                root3 * ux,
                root3 * uy,
                root3 * uz,
                root15 * ux * uy,
                root15 * uy * uz,
                0.5 * root5 * (3.0 * uz * uz - 1.0),
                root15 * ux * uz,
                0.5 * root15 * (ux * ux - uy * uy),
            ]
            for lm in range(9):
                for b in range(NB):
                    value = radial[b] if lm == 0 else radial[b] * angular[lm]
                    at = (lm * NB + b) * OCT + 16 * h
                    lhs[at : at + 16, t * 128 : (t + 1) * 128] = value.astype(bf16)
    for lm in range(9):
        summed = jnp.dot(lhs[lm * 256 : (lm + 1) * 256], cand[...], preferred_element_type=f32)
        message = summed[0:OCT] * rw[0:1]
        for b in range(1, NB):
            message = message + summed[b * OCT : (b + 1) * OCT] * rw[b : b + 1]
        sums_out(lm, message)
    return left


def mesh_kernel(
    state, base, frac, charge, count, codes_all, rw, tz_all, ty_all, fx_all, bx_all,
    hs, grads, near, hist, total, cols, lefts,
    hp, posbuf, rows, codes, tz, ty, fx, bx, wz, dwz, xt, yt, ys,
    s1, r1, s2, r2, s3, r3, s4, r4, s5, r5, grid, cand, lhs, extra, pick,
    send_sem, recv_sem, hsend, hrecv, lsem,
):
    ix, iy, iz = lax.axis_index("dx"), lax.axis_index("dy"), lax.axis_index("dz")
    here = {"dx": ix, "dy": iy, "dz": iz}
    barrier = pltpu.get_barrier_semaphore()

    for axis in ("dx", "dy", "dz"):

        def greet(s, carry, axis=axis):
            pl.semaphore_signal(
                barrier, inc=1, device_id={axis: lax.rem(here[axis] + s, 8)}, device_id_type=MESH
            )
            return carry

        lax.fori_loop(1, 8, greet, 0)

    local = [
        pltpu.make_async_copy(tz_all.at[iz], tz, lsem.at[0]),
        pltpu.make_async_copy(ty_all.at[iy], ty, lsem.at[1]),
        pltpu.make_async_copy(bx_all.at[ix], bx, lsem.at[2]),
        pltpu.make_async_copy(state, hs.at[pl.ds(1, 2), pl.ds(1, 2), pl.ds(1, 2)], lsem.at[3]),
        pltpu.make_async_copy(fx_all, fx, lsem.at[4]),
        pltpu.make_async_copy(codes_all, codes, lsem.at[5]),
    ]
    for copy in local:
        copy.start()

    gather_columns(base, frac, charge, count, (ix * MB, iy * MB, iz * MB), rows, cols, posbuf)
    hp[1:3, 1:3, 1:3] = posbuf[...]
    pl.semaphore_wait(barrier, 21)

    def halo(stage, axis, src_up, dst_up, src_down, dst_down):
        out = []
        for which in range(2):
            full = (hs, hp)[which]
            first = (state, posbuf)[which]
            up_src = first.at[src_up] if stage == 0 else full.at[src_up]
            down_src = first.at[src_down] if stage == 0 else full.at[src_down]
            for way, (src, dst, step) in enumerate(
                ((up_src, full.at[dst_up], 1), (down_src, full.at[dst_down], 7))
            ):
                n = stage * 4 + which * 2 + way
                out.append(
                    pltpu.make_async_remote_copy(
                        src_ref=src,
                        dst_ref=dst,
                        send_sem=hsend.at[n],
                        recv_sem=hrecv.at[n],
                        device_id={axis: lax.rem(here[axis] + step, 8)},
                        device_id_type=MESH,
                    )
                )
        return out

    mid = pl.ds(1, 2)
    full = pl.ds(0, 4)

    def one(n):
        return pl.ds(n, 1)

    halo_x = halo(0, "dx", (one(1),), (one(0), mid, mid), (one(0),), (one(3), mid, mid))
    halo_y = halo(
        1, "dy", (full, one(2), mid), (full, one(0), mid), (full, one(1), mid), (full, one(3), mid)
    )
    halo_z = halo(
        2, "dz", (full, full, one(2)), (full, full, one(0)), (full, full, one(1)), (full, full, one(3))
    )

    for copy in halo_x:
        copy.start()

    lane = lax.broadcasted_iota(jnp.int32, (ATOMS, 128), 1)
    cell = lane.astype(f32)
    half_cell = (lane % 64).astype(f32)

    def column(c):
        return jnp.broadcast_to(cols[:, lane_of(c) : lane_of(c) + 1], (ATOMS, 128))

    table, slope = spline_tables(column(2), column(5), cell)
    local[0].wait()
    wz[...] = dot_full(table[:, :WIN], tz[...])
    dwz[:, 0:128] = slope
    table, slope = spline_tables(column(1), column(4), half_cell)
    yt[...] = table
    ys[...] = slope
    table, slope = spline_tables(column(0), column(3), cell)
    xt[0:ATOMS] = table
    xt[ATOMS : 2 * ATOMS] = slope
    left = jnp.transpose(table * column(6))[:WIN]
    for k in range(KZW):
        s1[k] = dot_full(left, yt[...] * wz[:, k * 128 : (k + 1) * 128])

    def link(phase, axis, s, src, dst):
        return pltpu.make_async_remote_copy(
            src_ref=src,
            dst_ref=dst,
            send_sem=send_sem.at[phase, s],
            recv_sem=recv_sem.at[phase, s],
            device_id={axis: lax.rem(here[axis] + s, 8)},
            device_id_type=MESH,
        )

    def deal(phase, axis, s, sent, got):
        return link(phase, axis, s, sent.at[lax.rem(here[axis] + s, 8)], got.at[s])

    def share(phase, axis, s, sent, got, arriving):
        slot = lax.rem(here[axis] + 8 - s, 8) if arriving else here[axis]
        return link(phase, axis, s, sent, got.at[slot])

    def start_deal(phase, axis, sent, got):
        def body(s, carry):
            deal(phase, axis, s, sent, got).start()
            return carry

        lax.fori_loop(1, 8, body, 0)

    def wait_deal(phase, axis, sent, got):
        def body(s, carry):
            deal(phase, axis, s, sent, got).wait()
            return carry

        lax.fori_loop(1, 8, body, 0)
        total = sent[here[axis]]
        for s in range(1, 8):
            total = total + got[s]
        return total

    def start_share(phase, axis, sent, got):
        got[here[axis]] = sent[...]

        def body(s, carry):
            share(phase, axis, s, sent, got, False).start()
            return carry

        lax.fori_loop(1, 8, body, 0)

    def wait_share(phase, axis, sent, got):
        def body(s, carry):
            share(phase, axis, s, sent, got, True).wait()
            return carry

        lax.fori_loop(1, 8, body, 0)

    start_deal(0, "dz", s1, r1)
    local[3].wait()
    for copy in halo_x:
        copy.wait()
    for copy in halo_y:
        copy.start()
    local[1].wait()
    local[5].wait()
    count_pairs(codes, cols, hist, 0, 4)
    for copy in halo_y:
        copy.wait()
    for copy in halo_z:
        copy.start()
    spread = dot_full(wait_deal(0, "dz", s1, r1), ty[...])
    for p in range(8):
        s2[p] = spread[:, p * 128 : (p + 1) * 128]
    start_deal(1, "dy", s2, r2)
    count_pairs(codes, cols, hist, 4, 8)

    kx = lax.broadcasted_iota(jnp.int32, (EXT, 128), 0)
    lane_k = lax.broadcasted_iota(jnp.int32, (EXT, 128), 1)
    ky = iy * 32 + (lane_k % 64) % 32

    def folded(k):
        return jnp.where(2 * k >= EXT, k - EXT, k).astype(f32) / (cell_size * EXT)

    wave_z = (iz + 1).astype(f32) / (cell_size * EXT)
    wave_square = folded(kx) * folded(kx) + folded(ky) * folded(ky) + wave_z * wave_z
    volume = cell_size**3 * EXT * EXT * EXT
    green = (
        coulomb
        / (math.pi * volume)
        * jnp.exp(-(math.pi**2) / ewald_beta**2 * wave_square)
        / wave_square
    )
    sign = jnp.where(lane_k < 64, 1.0, -1.0).astype(f32)

    for copy in halo_z:
        copy.wait()

    def edges(octant, carry):
        line_up(octant, hs, cand)
        line_up_places(octant, hp, near, (ix, iy, iz))

        def keep(lm, message):
            total[lm, pl.ds(pl.multiple_of(octant * OCT, OCT), OCT), :] = message

        left = edge_pass(octant, cols, near, hist, rw, cand, lhs, extra, pick, keep)
        lefts[pl.ds(octant, 1), :] = jnp.broadcast_to(left, (1, 128))
        return carry

    lax.fori_loop(0, 2, edges, 0)
    s3[...] = wait_deal(1, "dy", s2, r2)
    start_share(2, "dx", s3, r3)
    lax.fori_loop(2, 4, edges, 0)
    dwz[...] = dot_full(dwz[:, 0:WIN], tz[...])
    local[2].wait()
    local[4].wait()
    wait_share(2, "dx", s3, r3)
    for d in range(8):
        grid[d * 32 : d * 32 + 8] = r3[d, 0:8] + r3[(d + 7) % 8, 32:40]
        grid[d * 32 + 8 : d * 32 + 32] = r3[d, 8:32]
    lined = grid[...]
    spec = dot_full(fx[0], lined) + dot_full(fx[1], sign * pltpu.roll(lined, 64, 1))
    scaled = spec * green
    s4[...] = dot_full(bx[0], scaled) - dot_full(bx[1], sign * pltpu.roll(scaled, 64, 1))
    start_share(3, "dy", s4, r4)
    lax.fori_loop(4, 6, edges, 0)
    wait_share(3, "dy", s4, r4)
    back = jnp.zeros((WIN, 128), f32)
    for p in range(8):
        back = back + lax.dot_general(
            r4[p],
            ty[:, p * 128 : (p + 1) * 128],
            (((1,), (1,)), ((), ())),
            precision=highest,
            preferred_element_type=f32,
        )
    s5[...] = back
    start_share(4, "dz", s5, r5)
    lax.fori_loop(6, 8, edges, 0)
    wait_share(4, "dz", s5, r5)
    along = jnp.zeros((ATOMS, 128), f32)
    along_z = jnp.zeros((ATOMS, 128), f32)
    tilted = jnp.zeros((ATOMS, 128), f32)
    for k in range(KZW):
        near = dot_full(xt[:, :WIN], r5[k])
        wave = wz[:, k * 128 : (k + 1) * 128]
        along = along + near[:ATOMS] * wave
        along_z = along_z + near[:ATOMS] * dwz[:, k * 128 : (k + 1) * 128]
        tilted = tilted + near[ATOMS:] * wave
    grad_x = jnp.sum(tilted * yt[...], axis=1, keepdims=True)
    grad_y = jnp.sum(along * ys[...], axis=1, keepdims=True)
    grad_z = jnp.sum(along_z * yt[...], axis=1, keepdims=True)
    scale = -(column(6) / cell_size) * 2.0
    grads[...] = scale * jnp.where(lane == 0, grad_x, jnp.where(lane == 1, grad_y, grad_z))


def mesh_call(state, base, frac, charge, count, codes, rw, tables):
    hbm_spec = pl.BlockSpec(memory_space=pltpu.HBM)
    vmem_spec = pl.BlockSpec(memory_space=pltpu.VMEM)
    block = (8, WIN, 128)
    return pl.pallas_call(
        mesh_kernel,
        out_shape=(
            jax.ShapeDtypeStruct((4, 4, 4, OCT, 128), bf16),
            jax.ShapeDtypeStruct((ATOMS, 128), f32),
            jax.ShapeDtypeStruct((8, 7, 8, 128), f32),
            jax.ShapeDtypeStruct((ATOMS * 8, 128), f32),
            jax.ShapeDtypeStruct((9, ATOMS, 128), f32),
            jax.ShapeDtypeStruct((ATOMS, 128), f32),
            jax.ShapeDtypeStruct((8, 128), f32),
        ),
        in_specs=[hbm_spec] + [vmem_spec] * 4 + [hbm_spec, vmem_spec] + [hbm_spec] * 4,
        out_specs=(vmem_spec,) * 7,
        scratch_shapes=[
            pltpu.VMEM((4, 4, 4, 8, 128), f32),
            pltpu.VMEM((2, 2, 2, 8, 128), f32),
            pltpu.VMEM((128, 128), f32),
            pltpu.VMEM((ATOMS, 128), jnp.int32),
            pltpu.VMEM((WIN, 1024), f32),
            pltpu.VMEM((128, 1024), f32),
            pltpu.VMEM((2, EXT, EXT), f32),
            pltpu.VMEM((2, WIN, EXT), f32),
            pltpu.VMEM((ATOMS, 1024), f32),
            pltpu.VMEM((ATOMS, 1024), f32),
            pltpu.VMEM((2 * ATOMS, 128), f32),
            pltpu.VMEM((ATOMS, 128), f32),
            pltpu.VMEM((ATOMS, 128), f32),
            pltpu.VMEM(block, f32),
            pltpu.VMEM(block, f32),
            pltpu.VMEM(block, f32),
            pltpu.VMEM(block, f32),
            pltpu.VMEM((WIN, 128), f32),
            pltpu.VMEM(block, f32),
            pltpu.VMEM((WIN, 128), f32),
            pltpu.VMEM(block, f32),
            pltpu.VMEM((WIN, 128), f32),
            pltpu.VMEM(block, f32),
            pltpu.VMEM((EXT, 128), f32),
            pltpu.VMEM((1024, 128), bf16),
            pltpu.VMEM((9 * 256, 1024), bf16),
            pltpu.VMEM((64, 896), bf16),
            pltpu.VMEM((128, 896), bf16),
            pltpu.SemaphoreType.DMA((5, 8)),
            pltpu.SemaphoreType.DMA((5, 8)),
            pltpu.SemaphoreType.DMA((12,)),
            pltpu.SemaphoreType.DMA((12,)),
            pltpu.SemaphoreType.DMA((6,)),
        ],
        compiler_params=pltpu.CompilerParams(
            collective_id=0, has_side_effects=True, vmem_limit_bytes=60 * 1024 * 1024
        ),
        name="mesh_forces",
    )(state, base, frac, charge, count, codes, rw, *tables)


def node_kernel(
    hs_in, near_in, hist_in, state, total_in, cols, lefts, rw, mix, fw, grads,
    node_out, force_out,
    cand, lhs, extra, pick, hs, near, hist, total, sem,
):
    def finish(octant, carry):
        rows = pl.ds(pl.multiple_of(octant * OCT, OCT), OCT)
        hist_rows = pl.ds(pl.multiple_of(octant * 256, 256), 256)

        @pl.when(jnp.max(lefts[pl.ds(octant, 1), :]) > 0.0)
        def _():
            line_up(octant, hs, cand)

            def add(lm, message):
                total[lm, rows, :] = total[lm, rows, :] + message

            def one_pass(again):
                hist[hist_rows, :] = jnp.maximum(hist[hist_rows, :] - 2.0, 0.0)
                left = edge_pass(octant, cols, near, hist, rw, cand, lhs, extra, pick, add)
                return jnp.max(left) > 0.0

            lax.while_loop(lambda again: again, one_pass, jnp.bool_(True))

        return carry

    total[...] = total_in[...]

    @pl.when(jnp.max(lefts[...]) > 0.0)
    def _():
        for n, (source, target) in enumerate(((hs_in, hs), (near_in, near), (hist_in, hist))):
            copy = pltpu.make_async_copy(source, target, sem.at[n])
            copy.start()
            copy.wait()
        lax.fori_loop(0, 8, finish, 0)

    def message(lm):
        return (total[lm] * (1.0 / math.sqrt(NBR))).astype(bf16)

    invariant = jnp.dot(message(0), mix[0], preferred_element_type=f32)
    power = jnp.zeros((ATOMS, 128), f32)
    for lm in range(4, 9):
        tensor = jnp.dot(message(lm), mix[2], preferred_element_type=f32)
        power = power + tensor * tensor
    invariant = invariant + power
    gating = jax.nn.sigmoid(invariant)
    node_out[...] = (state[...].astype(f32) + invariant * gating).astype(bf16)
    gate = gating * fw[...]
    lane = lax.broadcasted_iota(jnp.int32, (OCT, 128), 1)
    lined = jnp.zeros((OCT, 128), f32)
    for k in range(3):
        vector = jnp.dot(message(1 + k), mix[1], preferred_element_type=f32)
        push = jnp.sum(vector * gate, axis=1, keepdims=True) + grads[:, k : k + 1]
        for o in range(8):
            lined = jnp.where(lane == k * 8 + o, push[o * OCT : (o + 1) * OCT], lined)
    turned = jnp.transpose(jnp.concatenate([lined, jnp.zeros((96, 128), f32)], axis=0))
    for k in range(3):
        for cx in range(2):
            for cy in range(2):
                at = k * 8 + cx * 4 + cy * 2
                force_out[k, cx, cy] = turned[at : at + 2, 0:OCT]


def node_call(hs, near, hist, state, total, cols, lefts, rw, mix, fw, grads):
    vmem_spec = pl.BlockSpec(memory_space=pltpu.VMEM)
    return pl.pallas_call(
        node_kernel,
        out_shape=(
            jax.ShapeDtypeStruct((ATOMS, 128), bf16),
            jax.ShapeDtypeStruct((3, 2, 2, 2, OCT), f32),
        ),
        in_specs=[pl.BlockSpec(memory_space=pltpu.HBM)] * 3 + [vmem_spec] * 8,
        out_specs=(vmem_spec, vmem_spec),
        scratch_shapes=[
            pltpu.VMEM((1024, 128), bf16),
            pltpu.VMEM((9 * 256, 1024), bf16),
            pltpu.VMEM((64, 896), bf16),
            pltpu.VMEM((128, 896), bf16),
            pltpu.VMEM((4, 4, 4, OCT, 128), bf16),
            pltpu.VMEM((8, 7, 8, 128), f32),
            pltpu.VMEM((ATOMS * 8, 128), f32),
            pltpu.VMEM((9, ATOMS, 128), f32),
            pltpu.SemaphoreType.DMA((3,)),
        ],
        compiler_params=pltpu.CompilerParams(vmem_limit_bytes=60 * 1024 * 1024),
        name="node_update",
    )(hs, near, hist, state, total, cols, lefts, rw, mix, fw, grads)


def shards(tables, node_state, mesh_base, mesh_frac, charge, nbr_code, nbr_count,
           radial_weight, mix_weight, force_weight):
    hs, grads, near, hist, total, cols, lefts = mesh_call(
        node_state, mesh_base, mesh_frac, charge, nbr_count,
        nbr_code.reshape(ATOMS, NBR), radial_weight, tables,
    )
    node_next, forces = node_call(
        hs, near, hist, node_state.reshape(ATOMS, 128), total, cols, lefts, radial_weight, mix_weight,
        force_weight.reshape(1, 128), grads,
    )
    return (node_next.reshape(node_state.shape), forces)


def solution(mesh):
    placed = (
        P("dx", "dy", "dz", None, None),
        P(None, "dx", "dy", "dz", None),
        P(None, "dx", "dy", "dz", None),
        P("dx", "dy", "dz", None),
        P("dx", "dy", "dz", None, None),
        P("dx", "dy", "dz", None),
        P(),
        P(),
        P(),
    )
    tables = wave_tables()

    def run(*args):
        return shards(tuple(jnp.asarray(t) for t in tables), *args)

    return jax.shard_map(
        run,
        mesh=mesh,
        in_specs=placed,
        out_specs=(P("dx", "dy", "dz", None, None), P(None, "dx", "dy", "dz", None)),
        check_vma=False,
    )
```

```python
import functools
import math

import jax
import jax.numpy as jnp
import numpy as np
from jax import lax
from jax.experimental import pallas as pl
from jax.experimental.pallas import tpu as pltpu
from jax.sharding import PartitionSpec as P

NB = 8
NBR = 128
MB = 32
KZW = 8
OCT = 32
ATOMS = 8 * OCT
WIN = 40
EXT = 256

cell_size = 1.13
ewald_beta = 0.625
coulomb = 332.0637
sigma_low = 8.0
sigma_rate = 1.5
highest = lax.Precision.HIGHEST
MESH = pl.DeviceIdType.MESH
f32 = jnp.float32
bf16 = jnp.bfloat16


def wave_tables():
    cells = np.arange(WIN)
    angle = 2.0 * np.pi / EXT
    table_z = np.zeros((8, WIN, KZW, 2, 64))
    table_y = np.zeros((8, 2, 64, 8, 2, 64))
    back_x = np.zeros((8, 2, WIN, EXT))
    modes = np.arange(EXT)
    for d in range(8):
        at = d * MB + cells
        turn = angle * np.mod(at[:, None] * (1 + np.arange(KZW))[None, :], EXT)
        table_z[d, :, :, 0] = np.cos(turn)[:, :, None]
        table_z[d, :, :, 1] = -np.sin(turn)[:, :, None]
        turn = (angle * np.mod(at[:, None] * modes[None, :], EXT)).reshape(WIN, 8, 32)
        table_y[d, 0, :WIN, :, 0, :32] = np.cos(turn)
        table_y[d, 0, :WIN, :, 1, :32] = -np.sin(turn)
        table_y[d, 1, :WIN, :, 0, :32] = np.sin(turn)
        table_y[d, 1, :WIN, :, 1, :32] = np.cos(turn)
        turn = angle * np.mod(at[:, None] * modes[None, :], EXT)
        back_x[d, 0] = np.cos(turn)
        back_x[d, 1] = np.sin(turn)
    turn = angle * np.mod(modes[:, None] * modes[None, :], EXT)
    fore_x = np.stack([np.cos(turn), np.sin(turn)])
    return (
        table_z.reshape(8, WIN, KZW * 128).astype(np.float32),
        table_y.reshape(8, 128, 1024).astype(np.float32),
        fore_x.astype(np.float32),
        back_x.astype(np.float32),
    )


def dot_full(a, b):
    return jnp.dot(a, b, precision=highest, preferred_element_type=f32)


def spline_tables(base, frac, cell):
    left = 1.0 - frac
    square = frac * frac
    cube = square * frac
    weights = (
        left * left * left / 6.0,
        (3.0 * cube - 6.0 * square + 4.0) / 6.0,
        (-3.0 * cube + 3.0 * square + 3.0 * frac + 1.0) / 6.0,
        cube / 6.0,
    )
    slopes = (
        -0.5 * left * left,
        1.5 * square - 2.0 * frac,
        -1.5 * square + frac + 0.5,
        0.5 * square,
    )
    offset = cell - base
    table = jnp.zeros_like(offset)
    slope = jnp.zeros_like(offset)
    for t in range(4):
        hit = offset == float(t)
        table = jnp.where(hit, weights[t], table)
        slope = jnp.where(hit, slopes[t], slope)
    return table, slope


def top_power(count):
    power = count
    for bit in range(1, 8):
        power = jnp.where(count >= 2.0**bit, 2.0**bit, power)
    return power


def lane_of(quantity):
    return 8 * quantity


def gather_columns(base, frac, charge, count, anchor, rows, cols, posbuf):
    rows[...] = jnp.zeros_like(rows)
    for d in range(3):
        for cx in range(2):
            for cy in range(2):
                at = cx * 4 + cy * 2
                cells = base[d, cx, cy]
                part = frac[d, cx, cy]
                rows[d * 8 + at : d * 8 + at + 2, 0:OCT] = (cells - anchor[d]).astype(f32)
                rows[(3 + d) * 8 + at : (3 + d) * 8 + at + 2, 0:OCT] = part
                rows[(7 + d) * 8 + at : (7 + d) * 8 + at + 2, 0:OCT] = cells.astype(f32) + part
    for cx in range(2):
        for cy in range(2):
            at = cx * 4 + cy * 2
            rows[48 + at : 50 + at, 0:OCT] = charge[cx, cy]
            rows[80 + at : 82 + at, 0:OCT] = count[cx, cy].astype(f32)
    turned = jnp.transpose(rows[...])[0:OCT]
    for o in range(8):
        cols[o * OCT : (o + 1) * OCT] = pltpu.roll(turned, (128 - o) % 128, 1) if o else turned
        place = jnp.concatenate(
            [rows[(7 + d) * 8 + o : (7 + d) * 8 + o + 1] for d in range(3)] + [jnp.zeros((5, 128), f32)],
            axis=0,
        )
        place = place + pltpu.roll(place, 32, 1)
        posbuf[o // 4, o // 2 % 2, o % 2] = place + pltpu.roll(place, 64, 1)


def count_pairs(codes, cols, hist, first, last):
    sub8 = lax.broadcasted_iota(jnp.int32, (8, 128), 0)
    sub128 = lax.broadcasted_iota(jnp.int32, (128, 128), 0)
    slot = lax.broadcasted_iota(jnp.int32, (1, 128), 1).astype(f32)

    def count(g, c):
        for u in range(8):
            i = g * 8 + u
            row = codes[pl.ds(i, 1), :]
            live = slot < cols[pl.ds(i, 1), lane_of(10) : lane_of(10) + 1]
            row = jnp.where(live, row, 1023)
            high = jnp.broadcast_to(row >> 7, (8, 128))
            low = jnp.broadcast_to(row & 127, (128, 128))
            a = jnp.where(high == sub8, 1.0, 0.0).astype(bf16)
            b = jnp.where(low == sub128, 1.0, 0.0).astype(bf16)
            hist[pl.ds(pl.multiple_of(i * 8, 8), 8), :] = lax.dot_general(
                a, b, (((1,), (1,)), ((), ())), preferred_element_type=f32
            )
        return c

    lax.fori_loop(first * 4, last * 4, count, 0)


def line_up(octant, hs, cand):
    cx, cy, cz = octant // 4, octant // 2 % 2, octant % 2
    for side in range(27):
        hx, hy, hz = cx + side // 9, cy + side // 3 % 3, cz + side % 3
        cand[side * 32 : side * 32 + 32] = hs[hx, hy, hz]
    cand[864:896] = jnp.zeros((32, 128), bf16)


def line_up_places(octant, hp, near, index):
    cx, cy, cz = octant // 4, octant // 2 % 2, octant % 2
    lane = lax.broadcasted_iota(jnp.int32, (8, 128), 1)
    sub8 = lax.broadcasted_iota(jnp.int32, (8, 128), 0)

    def wrap(here, h):
        reach = 2 * here + h - 1
        return jnp.where(reach < 0, -float(EXT), jnp.where(reach > 15, float(EXT), 0.0)).astype(f32)

    wrap_x = [wrap(index[0], cx + n) for n in range(3)]
    wrap_y = [wrap(index[1], cy + n) for n in range(3)]
    wrap_z = [wrap(index[2], cz + n) for n in range(3)]
    tiles = []
    for side in range(27):
        nx, ny, nz = side // 9, side // 3 % 3, side % 3
        shift = jnp.where(sub8 == 0, wrap_x[nx], jnp.where(sub8 == 1, wrap_y[ny], wrap_z[nz]))
        tiles.append(hp[cx + nx, cy + ny, cz + nz] + shift)
    tiles.append(tiles[26])
    for t in range(7):
        four = tiles[4 * t : 4 * t + 4]
        near[octant, t] = jnp.where(
            lane < 32, four[0], jnp.where(lane < 64, four[1], jnp.where(lane < 96, four[2], four[3]))
        )


def edge_pass(octant, cols, near, hist, rw, cand, lhs, extra, pick, sums_out):
    sub8 = lax.broadcasted_iota(jnp.int32, (8, 128), 0)
    sub128 = lax.broadcasted_iota(jnp.int32, (128, 128), 0)
    lane128 = lax.broadcasted_iota(jnp.int32, (128, 128), 1)
    lane32 = lax.broadcasted_iota(jnp.int32, (OCT, 128), 1)
    before = jnp.where(sub128 < lane128, 1.0, 0.0).astype(bf16)
    ones = jnp.ones((128, 128), bf16)
    place_id = (sub128 & 63).astype(f32)
    root3, root5, root15 = math.sqrt(3.0), math.sqrt(5.0), math.sqrt(15.0)
    rates = [
        -(cell_size**2) / (sigma_low * sigma_rate**b) ** 2 / math.log(2.0) for b in range(NB)
    ]
    row0 = pl.multiple_of(octant * OCT, OCT)
    hist0 = octant * 256

    def listed(t):
        return hist[pl.ds(hist0 + t, OCT, 8), :]

    flags = jnp.zeros((8, 128), f32)
    for t in range(7):
        at = slice(t * 128, (t + 1) * 128)
        place = near[octant, t]
        first = place.astype(bf16).astype(f32)
        rest = place - first
        second = rest.astype(bf16).astype(f32)
        extra[32:48, at] = jnp.concatenate([first, second], axis=0).astype(bf16)
        extra[48:64, at] = jnp.concatenate([rest - second, jnp.zeros_like(rest)], axis=0).astype(bf16)
        over = jnp.maximum(listed(t) - 2.0, 0.0)
        extra[0:OCT, at] = over.astype(bf16)
        flag = jnp.where(jnp.max(over, axis=0, keepdims=True) > 0.0, 1.0, 0.0)
        flags = jnp.where(sub8 == t, flag, flags)
    flags_b = flags.astype(bf16)
    rank = jnp.dot(flags_b, before, preferred_element_type=f32)
    sums = jnp.dot(flags_b, ones, preferred_element_type=f32)
    offset = jnp.zeros((1, 128), f32)
    for t in range(7):
        key = jnp.where(flags[t : t + 1] > 0.0, rank[t : t + 1] + offset, -1.0)
        pick[:, t * 128 : (t + 1) * 128] = jnp.where(key == place_id, 1.0, 0.0).astype(bf16)
        offset = offset + sums[t : t + 1]
    picked = lax.dot_general(
        extra[...], pick[...], (((1,), (1,)), ((), ())), preferred_element_type=f32
    )
    cand[896:1024] = jnp.dot(pick[...], cand[0:896], preferred_element_type=f32).astype(bf16)
    more = picked[0:OCT]
    power = top_power(more)
    second = top_power(more - power)
    left = jnp.max(jnp.maximum(more - power - second, offset - 64.0), axis=0, keepdims=True)
    left = jnp.max(left, axis=1, keepdims=True)
    spare = jnp.where(left > 0.0, 0.0, jnp.where(lane32 < 64, power, second))
    spare_place = picked[32:40] + picked[40:48] + picked[48:56]
    own = [
        jnp.broadcast_to(cols[pl.ds(row0, OCT), lane_of(7 + d) : lane_of(7 + d) + 1], (OCT, 128))
        for d in range(3)
    ]
    for t in range(8):
        place = spare_place if t == 7 else near[octant, t]
        times_all = spare if t == 7 else jnp.minimum(listed(t), 2.0)
        for h in range(2):
            rows = slice(16 * h, 16 * h + 16)
            delta = [place[d : d + 1] - own[d][rows] for d in range(3)]
            square = delta[0] * delta[0] + delta[1] * delta[1] + delta[2] * delta[2]
            inv = lax.rsqrt(square + 1.0)
            ux, uy, uz = (d * inv for d in delta)
            times = times_all[rows]
            radial = [jnp.exp2(square * rates[b]) * times for b in range(NB)]
            angular = [
                None,
                root3 * ux,
                root3 * uy,
                root3 * uz,
                root15 * ux * uy,
                root15 * uy * uz,
                0.5 * root5 * (3.0 * uz * uz - 1.0),
                root15 * ux * uz,
                0.5 * root15 * (ux * ux - uy * uy),
            ]
            for lm in range(9):
                for b in range(NB):
                    value = radial[b] if lm == 0 else radial[b] * angular[lm]
                    at = (lm * NB + b) * OCT + 16 * h
                    lhs[at : at + 16, t * 128 : (t + 1) * 128] = value.astype(bf16)
    for lm in range(9):
        summed = jnp.dot(lhs[lm * 256 : (lm + 1) * 256], cand[...], preferred_element_type=f32)
        message = summed[0:OCT] * rw[0:1]
        for b in range(1, NB):
            message = message + summed[b * OCT : (b + 1) * OCT] * rw[b : b + 1]
        sums_out(lm, message)
    return left


def mesh_kernel(
    state, base, frac, charge, count, codes_all, rw, tz_all, ty_all, fx_all, bx_all,
    hs, grads, near, hist, total, cols, lefts,
    hp, posbuf, rows, codes, tz, ty, fx, bx, wz, dwz, xt, yt, ys,
    s1, r1, s2, r2, s3, r3, s4, r4, s5, r5, grid, cand, lhs, extra, pick,
    send_sem, recv_sem, hsend, hrecv, lsem,
):
    ix, iy, iz = lax.axis_index("dx"), lax.axis_index("dy"), lax.axis_index("dz")
    here = {"dx": ix, "dy": iy, "dz": iz}
    barrier = pltpu.get_barrier_semaphore()

    for axis in ("dx", "dy", "dz"):

        def greet(s, carry, axis=axis):
            pl.semaphore_signal(
                barrier, inc=1, device_id={axis: lax.rem(here[axis] + s, 8)}, device_id_type=MESH
            )
            return carry

        lax.fori_loop(1, 8, greet, 0)

    local = [
        pltpu.make_async_copy(tz_all.at[iz], tz, lsem.at[0]),
        pltpu.make_async_copy(ty_all.at[iy], ty, lsem.at[1]),
        pltpu.make_async_copy(bx_all.at[ix], bx, lsem.at[2]),
        pltpu.make_async_copy(state, hs.at[pl.ds(1, 2), pl.ds(1, 2), pl.ds(1, 2)], lsem.at[3]),
        pltpu.make_async_copy(fx_all, fx, lsem.at[4]),
        pltpu.make_async_copy(codes_all, codes, lsem.at[5]),
    ]
    for copy in local:
        copy.start()

    gather_columns(base, frac, charge, count, (ix * MB, iy * MB, iz * MB), rows, cols, posbuf)
    hp[1:3, 1:3, 1:3] = posbuf[...]
    lane = lax.broadcasted_iota(jnp.int32, (ATOMS, 128), 1)
    cell = lane.astype(f32)
    half_cell = (lane % 64).astype(f32)

    def column(c):
        return jnp.broadcast_to(cols[:, lane_of(c) : lane_of(c) + 1], (ATOMS, 128))

    table, slope = spline_tables(column(2), column(5), cell)
    local[0].wait()
    wz[...] = dot_full(table[:, :WIN], tz[...])
    dwz[:, 0:128] = slope
    table, slope = spline_tables(column(1), column(4), half_cell)
    yt[...] = table
    ys[...] = slope
    table, slope = spline_tables(column(0), column(3), cell)
    xt[0:ATOMS] = table
    xt[ATOMS : 2 * ATOMS] = slope
    left = jnp.transpose(table * column(6))[:WIN]
    for k in range(KZW):
        s1[k] = dot_full(left, yt[...] * wz[:, k * 128 : (k + 1) * 128])

    pl.semaphore_wait(barrier, 21)

    def halo(stage, axis, src_up, dst_up, src_down, dst_down):
        out = []
        for which in range(2):
            full = (hs, hp)[which]
            first = (state, posbuf)[which]
            up_src = first.at[src_up] if stage == 0 else full.at[src_up]
            down_src = first.at[src_down] if stage == 0 else full.at[src_down]
            for way, (src, dst, step) in enumerate(
                ((up_src, full.at[dst_up], 1), (down_src, full.at[dst_down], 7))
            ):
                n = stage * 4 + which * 2 + way
                out.append(
                    pltpu.make_async_remote_copy(
                        src_ref=src,
                        dst_ref=dst,
                        send_sem=hsend.at[n],
                        recv_sem=hrecv.at[n],
                        device_id={axis: lax.rem(here[axis] + step, 8)},
                        device_id_type=MESH,
                    )
                )
        return out

    mid = pl.ds(1, 2)
    full = pl.ds(0, 4)

    def one(n):
        return pl.ds(n, 1)

    halo_x = halo(0, "dx", (one(1),), (one(0), mid, mid), (one(0),), (one(3), mid, mid))
    halo_y = halo(
        1, "dy", (full, one(2), mid), (full, one(0), mid), (full, one(1), mid), (full, one(3), mid)
    )
    halo_z = halo(
        2, "dz", (full, full, one(2)), (full, full, one(0)), (full, full, one(1)), (full, full, one(3))
    )

    for copy in halo_x:
        copy.start()

    def link(phase, axis, s, src, dst):
        return pltpu.make_async_remote_copy(
            src_ref=src,
            dst_ref=dst,
            send_sem=send_sem.at[phase, s],
            recv_sem=recv_sem.at[phase, s],
            device_id={axis: lax.rem(here[axis] + s, 8)},
            device_id_type=MESH,
        )

    def deal(phase, axis, s, sent, got):
        return link(phase, axis, s, sent.at[lax.rem(here[axis] + s, 8)], got.at[s])

    def share(phase, axis, s, sent, got, arriving):
        slot = lax.rem(here[axis] + 8 - s, 8) if arriving else here[axis]
        return link(phase, axis, s, sent, got.at[slot])

    def start_deal(phase, axis, sent, got):
        def body(s, carry):
            deal(phase, axis, s, sent, got).start()
            return carry

        lax.fori_loop(1, 8, body, 0)

    def wait_deal(phase, axis, sent, got):
        def body(s, carry):
            deal(phase, axis, s, sent, got).wait()
            return carry

        lax.fori_loop(1, 8, body, 0)
        total = sent[here[axis]]
        for s in range(1, 8):
            total = total + got[s]
        return total

    def start_share(phase, axis, sent, got):
        got[here[axis]] = sent[...]

        def body(s, carry):
            share(phase, axis, s, sent, got, False).start()
            return carry

        lax.fori_loop(1, 8, body, 0)

    def wait_share(phase, axis, sent, got):
        def body(s, carry):
            share(phase, axis, s, sent, got, True).wait()
            return carry

        lax.fori_loop(1, 8, body, 0)

    start_deal(0, "dz", s1, r1)
    local[3].wait()
    local[5].wait()
    count_pairs(codes, cols, hist, 0, 2)
    for copy in halo_x:
        copy.wait()
    for copy in halo_y:
        copy.start()
    local[1].wait()
    count_pairs(codes, cols, hist, 2, 5)
    for copy in halo_y:
        copy.wait()
    for copy in halo_z:
        copy.start()
    spread = dot_full(wait_deal(0, "dz", s1, r1), ty[...])
    for p in range(8):
        s2[p] = spread[:, p * 128 : (p + 1) * 128]
    start_deal(1, "dy", s2, r2)
    count_pairs(codes, cols, hist, 5, 8)
    dwz[...] = dot_full(dwz[:, 0:WIN], tz[...])

    kx = lax.broadcasted_iota(jnp.int32, (EXT, 128), 0)
    lane_k = lax.broadcasted_iota(jnp.int32, (EXT, 128), 1)
    ky = iy * 32 + (lane_k % 64) % 32

    def folded(k):
        return jnp.where(2 * k >= EXT, k - EXT, k).astype(f32) / (cell_size * EXT)

    wave_z = (iz + 1).astype(f32) / (cell_size * EXT)
    wave_square = folded(kx) * folded(kx) + folded(ky) * folded(ky) + wave_z * wave_z
    volume = cell_size**3 * EXT * EXT * EXT
    green = (
        coulomb
        / (math.pi * volume)
        * jnp.exp(-(math.pi**2) / ewald_beta**2 * wave_square)
        / wave_square
    )
    sign = jnp.where(lane_k < 64, 1.0, -1.0).astype(f32)

    for copy in halo_z:
        copy.wait()

    def edges(octant, carry):
        line_up(octant, hs, cand)
        line_up_places(octant, hp, near, (ix, iy, iz))

        def keep(lm, message):
            total[lm, pl.ds(pl.multiple_of(octant * OCT, OCT), OCT), :] = message

        left = edge_pass(octant, cols, near, hist, rw, cand, lhs, extra, pick, keep)
        lefts[pl.ds(octant, 1), :] = jnp.broadcast_to(left, (1, 128))
        return carry

    lax.fori_loop(0, 1, edges, 0)
    s3[...] = wait_deal(1, "dy", s2, r2)
    start_share(2, "dx", s3, r3)
    lax.fori_loop(1, 3, edges, 0)
    local[2].wait()
    local[4].wait()
    wait_share(2, "dx", s3, r3)
    for d in range(8):
        grid[d * 32 : d * 32 + 8] = r3[d, 0:8] + r3[(d + 7) % 8, 32:40]
        grid[d * 32 + 8 : d * 32 + 32] = r3[d, 8:32]
    lined = grid[...]
    spec = dot_full(fx[0], lined) + dot_full(fx[1], sign * pltpu.roll(lined, 64, 1))
    scaled = spec * green
    s4[...] = dot_full(bx[0], scaled) - dot_full(bx[1], sign * pltpu.roll(scaled, 64, 1))
    start_share(3, "dy", s4, r4)
    lax.fori_loop(3, 6, edges, 0)
    wait_share(3, "dy", s4, r4)
    back = jnp.zeros((WIN, 128), f32)
    for p in range(8):
        back = back + lax.dot_general(
            r4[p],
            ty[:, p * 128 : (p + 1) * 128],
            (((1,), (1,)), ((), ())),
            precision=highest,
            preferred_element_type=f32,
        )
    s5[...] = back
    start_share(4, "dz", s5, r5)
    lax.fori_loop(6, 8, edges, 0)
    wait_share(4, "dz", s5, r5)
    along = jnp.zeros((ATOMS, 128), f32)
    along_z = jnp.zeros((ATOMS, 128), f32)
    tilted = jnp.zeros((ATOMS, 128), f32)
    for k in range(KZW):
        near = dot_full(xt[:, :WIN], r5[k])
        wave = wz[:, k * 128 : (k + 1) * 128]
        along = along + near[:ATOMS] * wave
        along_z = along_z + near[:ATOMS] * dwz[:, k * 128 : (k + 1) * 128]
        tilted = tilted + near[ATOMS:] * wave
    grad_x = jnp.sum(tilted * yt[...], axis=1, keepdims=True)
    grad_y = jnp.sum(along * ys[...], axis=1, keepdims=True)
    grad_z = jnp.sum(along_z * yt[...], axis=1, keepdims=True)
    scale = -(column(6) / cell_size) * 2.0
    grads[...] = scale * jnp.where(lane == 0, grad_x, jnp.where(lane == 1, grad_y, grad_z))


def mesh_call(state, base, frac, charge, count, codes, rw, tables):
    hbm_spec = pl.BlockSpec(memory_space=pltpu.HBM)
    vmem_spec = pl.BlockSpec(memory_space=pltpu.VMEM)
    block = (8, WIN, 128)
    return pl.pallas_call(
        mesh_kernel,
        out_shape=(
            jax.ShapeDtypeStruct((4, 4, 4, OCT, 128), bf16),
            jax.ShapeDtypeStruct((ATOMS, 128), f32),
            jax.ShapeDtypeStruct((8, 7, 8, 128), f32),
            jax.ShapeDtypeStruct((ATOMS * 8, 128), f32),
            jax.ShapeDtypeStruct((9, ATOMS, 128), f32),
            jax.ShapeDtypeStruct((ATOMS, 128), f32),
            jax.ShapeDtypeStruct((8, 128), f32),
        ),
        in_specs=[hbm_spec] + [vmem_spec] * 4 + [hbm_spec, vmem_spec] + [hbm_spec] * 4,
        out_specs=(vmem_spec,) * 7,
        scratch_shapes=[
            pltpu.VMEM((4, 4, 4, 8, 128), f32),
            pltpu.VMEM((2, 2, 2, 8, 128), f32),
            pltpu.VMEM((128, 128), f32),
            pltpu.VMEM((ATOMS, 128), jnp.int32),
            pltpu.VMEM((WIN, 1024), f32),
            pltpu.VMEM((128, 1024), f32),
            pltpu.VMEM((2, EXT, EXT), f32),
            pltpu.VMEM((2, WIN, EXT), f32),
            pltpu.VMEM((ATOMS, 1024), f32),
            pltpu.VMEM((ATOMS, 1024), f32),
            pltpu.VMEM((2 * ATOMS, 128), f32),
            pltpu.VMEM((ATOMS, 128), f32),
            pltpu.VMEM((ATOMS, 128), f32),
            pltpu.VMEM(block, f32),
            pltpu.VMEM(block, f32),
            pltpu.VMEM(block, f32),
            pltpu.VMEM(block, f32),
            pltpu.VMEM((WIN, 128), f32),
            pltpu.VMEM(block, f32),
            pltpu.VMEM((WIN, 128), f32),
            pltpu.VMEM(block, f32),
            pltpu.VMEM((WIN, 128), f32),
            pltpu.VMEM(block, f32),
            pltpu.VMEM((EXT, 128), f32),
            pltpu.VMEM((1024, 128), bf16),
            pltpu.VMEM((9 * 256, 1024), bf16),
            pltpu.VMEM((64, 896), bf16),
            pltpu.VMEM((128, 896), bf16),
            pltpu.SemaphoreType.DMA((5, 8)),
            pltpu.SemaphoreType.DMA((5, 8)),
            pltpu.SemaphoreType.DMA((12,)),
            pltpu.SemaphoreType.DMA((12,)),
            pltpu.SemaphoreType.DMA((6,)),
        ],
        compiler_params=pltpu.CompilerParams(
            collective_id=0, has_side_effects=True, vmem_limit_bytes=60 * 1024 * 1024
        ),
        name="mesh_forces",
    )(state, base, frac, charge, count, codes, rw, *tables)


def node_kernel(
    hs_in, near_in, hist_in, state, total_in, cols, lefts, rw, mix, fw, grads,
    node_out, force_out,
    cand, lhs, extra, pick, hs, near, hist, total, sem,
):
    def finish(octant, carry):
        rows = pl.ds(pl.multiple_of(octant * OCT, OCT), OCT)
        hist_rows = pl.ds(pl.multiple_of(octant * 256, 256), 256)

        @pl.when(jnp.max(lefts[pl.ds(octant, 1), :]) > 0.0)
        def _():
            line_up(octant, hs, cand)

            def add(lm, message):
                total[lm, rows, :] = total[lm, rows, :] + message

            def one_pass(again):
                hist[hist_rows, :] = jnp.maximum(hist[hist_rows, :] - 2.0, 0.0)
                left = edge_pass(octant, cols, near, hist, rw, cand, lhs, extra, pick, add)
                return jnp.max(left) > 0.0

            lax.while_loop(lambda again: again, one_pass, jnp.bool_(True))

        return carry

    total[...] = total_in[...]

    @pl.when(jnp.max(lefts[...]) > 0.0)
    def _():
        for n, (source, target) in enumerate(((hs_in, hs), (near_in, near), (hist_in, hist))):
            copy = pltpu.make_async_copy(source, target, sem.at[n])
            copy.start()
            copy.wait()
        lax.fori_loop(0, 8, finish, 0)

    def message(lm):
        return (total[lm] * (1.0 / math.sqrt(NBR))).astype(bf16)

    invariant = jnp.dot(message(0), mix[0], preferred_element_type=f32)
    power = jnp.zeros((ATOMS, 128), f32)
    for lm in range(4, 9):
        tensor = jnp.dot(message(lm), mix[2], preferred_element_type=f32)
        power = power + tensor * tensor
    invariant = invariant + power
    gating = jax.nn.sigmoid(invariant)
    node_out[...] = (state[...].astype(f32) + invariant * gating).astype(bf16)
    gate = gating * fw[...]
    lane = lax.broadcasted_iota(jnp.int32, (OCT, 128), 1)
    lined = jnp.zeros((OCT, 128), f32)
    for k in range(3):
        vector = jnp.dot(message(1 + k), mix[1], preferred_element_type=f32)
        push = jnp.sum(vector * gate, axis=1, keepdims=True) + grads[:, k : k + 1]
        for o in range(8):
            lined = jnp.where(lane == k * 8 + o, push[o * OCT : (o + 1) * OCT], lined)
    turned = jnp.transpose(jnp.concatenate([lined, jnp.zeros((96, 128), f32)], axis=0))
    for k in range(3):
        for cx in range(2):
            for cy in range(2):
                at = k * 8 + cx * 4 + cy * 2
                force_out[k, cx, cy] = turned[at : at + 2, 0:OCT]


def node_call(hs, near, hist, state, total, cols, lefts, rw, mix, fw, grads):
    vmem_spec = pl.BlockSpec(memory_space=pltpu.VMEM)
    return pl.pallas_call(
        node_kernel,
        out_shape=(
            jax.ShapeDtypeStruct((ATOMS, 128), bf16),
            jax.ShapeDtypeStruct((3, 2, 2, 2, OCT), f32),
        ),
        in_specs=[pl.BlockSpec(memory_space=pltpu.HBM)] * 3 + [vmem_spec] * 8,
        out_specs=(vmem_spec, vmem_spec),
        scratch_shapes=[
            pltpu.VMEM((1024, 128), bf16),
            pltpu.VMEM((9 * 256, 1024), bf16),
            pltpu.VMEM((64, 896), bf16),
            pltpu.VMEM((128, 896), bf16),
            pltpu.VMEM((4, 4, 4, OCT, 128), bf16),
            pltpu.VMEM((8, 7, 8, 128), f32),
            pltpu.VMEM((ATOMS * 8, 128), f32),
            pltpu.VMEM((9, ATOMS, 128), f32),
            pltpu.SemaphoreType.DMA((3,)),
        ],
        compiler_params=pltpu.CompilerParams(vmem_limit_bytes=60 * 1024 * 1024),
        name="node_update",
    )(hs, near, hist, state, total, cols, lefts, rw, mix, fw, grads)


def shards(tables, node_state, mesh_base, mesh_frac, charge, nbr_code, nbr_count,
           radial_weight, mix_weight, force_weight):
    hs, grads, near, hist, total, cols, lefts = mesh_call(
        node_state, mesh_base, mesh_frac, charge, nbr_count,
        nbr_code.reshape(ATOMS, NBR), radial_weight, tables,
    )
    node_next, forces = node_call(
        hs, near, hist, node_state.reshape(ATOMS, 128), total, cols, lefts, radial_weight, mix_weight,
        force_weight.reshape(1, 128), grads,
    )
    return (node_next.reshape(node_state.shape), forces)


def solution(mesh):
    placed = (
        P("dx", "dy", "dz", None, None),
        P(None, "dx", "dy", "dz", None),
        P(None, "dx", "dy", "dz", None),
        P("dx", "dy", "dz", None),
        P("dx", "dy", "dz", None, None),
        P("dx", "dy", "dz", None),
        P(),
        P(),
        P(),
    )
    tables = wave_tables()

    def run(*args):
        return shards(tuple(jnp.asarray(t) for t in tables), *args)

    return jax.shard_map(
        run,
        mesh=mesh,
        in_specs=placed,
        out_specs=(P("dx", "dy", "dz", None, None), P(None, "dx", "dy", "dz", None)),
        check_vma=False,
    )
```
